256 devices in a mesh: sector: 16 (over y, x), mode: 16 (over z, core).
Axes of the slice: x: 4, y: 4, z: 8, core: 2. Of those that a mesh axis runs over, the one named last changes fastest.
Arguments:
- pressure: bfloat16 [64, 256, 16384], P('sector', None, 'mode'), may hold values from -6 to 6
- basis: bfloat16 [16384, 1024], P('mode'), may hold values from -0.0625 to 0.0625
- recovery: bfloat16 [1024, 16384], P(None, 'mode'), may hold values from -0.1875 to 0.1875
- omega: float32 [33, 1024], P(None, 'mode'), may hold values from 0.5 to 4
- damping: float32 [33, 1024], P(None, 'mode'), may hold values from 0.1 to 0.4
- harmonic: int32 [256], replicated, may hold values from 1 to 16
Outputs:
- stress_re: bfloat16 [64, 256, 16384], P('sector', None, 'mode')
- stress_im: bfloat16 [64, 256, 16384], P('sector', None, 'mode')
The draws below stay inside these ranges and needn't reach their ends.
All inputs are finite; a program needn't handle non-finite values.
Results may differ from the reference program's by a relative error of at most 0.027.
Values may be sent and summed in bfloat16 or wider, within the bound.
A program may use at most 64 MiB of HBM per device.

```python
import math
import jax
import jax.numpy as jnp
from jax import lax

SECTORS = 64
MODES = 1024
DIAMS = 33
SAMPLES = 256
NODES = 16384
REC_NODES = 16384


def touch_ends(array, own_key, least, top_value):
    place = [jax.random.randint(jax.random.fold_in(own_key, axis), (), 0, length) for axis, length in enumerate(array.shape)]
    longest = array.shape.index(max(array.shape))
    next_to = place[:longest] + [(place[longest] + 1) % array.shape[longest]] + place[longest + 1:]
    return array.at[tuple(place)].set(least).at[tuple(next_to)].set(top_value)


def raised(drawn, rng, source, target, shards_of, factor):
    owner, partner = [(jnp.arange(drawn.shape[dim]) // (drawn.shape[dim] // shards_of)).reshape([-1 if axis == dim else 1 for axis in range(drawn.ndim)]) for dim in (source, target)]
    chosen = jax.random.permutation(rng, shards_of)[partner]
    strong = (owner == chosen) | (owner == (partner + shards_of // 2) % shards_of)
    return jnp.where(strong, factor * drawn, drawn)


def steps_of(key, dims, pieces, least, high):
    def one(position, parts):
        heights = jax.random.uniform(jax.random.fold_in(jax.random.fold_in(key, 6), position), (parts,), jnp.float32, least / len(pieces), high / len(pieces))
        return jnp.repeat(jnp.exp(heights), dims[position] // parts).reshape((-1,) + (1,) * (len(dims) - position - 1))

    loudness = one(*pieces[0])
    for cut in pieces[1:]:
        loudness = loudness * one(*cut)
    return loudness


def centred(stream_key, extent, spread, limit, cuts=(), kind=jnp.bfloat16):
    result = jax.random.normal(stream_key, extent, jnp.float32) * spread
    if len(cuts) > 0:
        result = steps_of(stream_key, extent, cuts, -0.22, 0.18) * result
    return jnp.clip(result, min=-limit, max=limit).astype(kind)


def heavy_noise(stream_key, dims, deviation, bound, cuts, heavy, kind=jnp.bfloat16):
    result = deviation * jax.random.normal(stream_key, dims, jnp.float32)
    if cuts:
        result = result * steps_of(stream_key, dims, cuts, -0.22, 0.18)
    return jnp.clip(raised(result, jax.random.fold_in(stream_key, 3), *heavy), -bound, bound).astype(kind)


def setup_inputs(seed: int = 0) -> dict:
    key_of = jax.random.split(jax.random.key(seed), 7)
    return {
        "pressure": centred(key_of[0], (SECTORS, SAMPLES, NODES), 1.0, 6.0, ((0, 16), (2, 16))),
        "basis": heavy_noise(key_of[1], (NODES, MODES), NODES ** -0.5, 0.0625, ((0, 16),), (0, 1, 16, 2.0)),
        "recovery": centred(key_of[2], (MODES, REC_NODES), MODES ** -0.5, 0.1875, ((1, 16),)),
        "omega": jnp.clip(jnp.exp(math.log(4.0) - 2.0794415 * jax.random.uniform(key_of[3], (DIAMS, MODES), jnp.float32) ** steps_of(key_of[3], (DIAMS, MODES), ((1, 16),), -0.2, 0.2)), 0.5, 4.0),
        "damping": jnp.clip(jnp.exp(math.log(0.4) - 1.3862944 * jax.random.uniform(key_of[4], (DIAMS, MODES), jnp.float32) ** steps_of(key_of[4], (DIAMS, MODES), ((1, 16),), -0.2, 0.2)), 0.1, 0.4),
        "harmonic": touch_ends(jax.random.randint(key_of[5], (SAMPLES,), 1, 17), jax.random.fold_in(key_of[5], 1), 1, 16).astype(jnp.int32),
    }


def phase_tables(sector_count):
    wave_index = jnp.arange(sector_count, dtype=jnp.int32)
    phases = (wave_index[:, None] * wave_index[None, :]) % sector_count
    angles = (2.0 * math.pi / sector_count) * phases.astype(jnp.float32)
    return jnp.cos(angles), jnp.sin(angles)


def reference(pressure, basis, recovery, omega, damping, harmonic):
    high = lax.Precision.HIGHEST
    loads = jnp.dot(pressure.reshape(SECTORS * SAMPLES, NODES), basis, preferred_element_type=jnp.float32)
    rounded = lax.optimization_barrier(loads.astype(jnp.bfloat16))
    modal = rounded.astype(jnp.float32).reshape(SECTORS, SAMPLES, MODES)
    cos_table, sine_table = phase_tables(SECTORS)
    spec_re = jnp.einsum("ks,stm->ktm", cos_table, modal, precision=high)
    spec_im = -jnp.einsum("ks,stm->ktm", sine_table, modal, precision=high)
    freq_wave = jnp.concatenate([omega, omega[-2:0:-1]], 0)[:, None, :]
    damp_wave = jnp.concatenate([damping, damping[-2:0:-1]], 0)[:, None, :]
    drive = (0.25 * harmonic.astype(jnp.float32))[None, :, None]
    stiff_part = freq_wave * freq_wave - drive * drive
    loss_part = 2.0 * damp_wave * freq_wave * drive
    magnitude = stiff_part * stiff_part + loss_part * loss_part
    recv_re = stiff_part / magnitude
    recv_im = -loss_part / magnitude
    resp_re = recv_re * spec_re - recv_im * spec_im
    resp_im = recv_re * spec_im + recv_im * spec_re
    back_re = (jnp.einsum("ks,ktm->stm", cos_table, resp_re, precision=high) - jnp.einsum("ks,ktm->stm", sine_table, resp_im, precision=high)) / SECTORS
    back_im = (jnp.einsum("ks,ktm->stm", sine_table, resp_re, precision=high) + jnp.einsum("ks,ktm->stm", cos_table, resp_im, precision=high)) / SECTORS
    sector_re = back_re.astype(jnp.bfloat16).reshape(SECTORS * SAMPLES, MODES)
    sector_im = back_im.astype(jnp.bfloat16).reshape(SECTORS * SAMPLES, MODES)
    stress_re = jnp.dot(sector_re, recovery, preferred_element_type=jnp.float32).astype(jnp.bfloat16)
    stress_im = jnp.dot(sector_im, recovery, preferred_element_type=jnp.float32).astype(jnp.bfloat16)
    return stress_re.reshape(SECTORS, SAMPLES, REC_NODES), stress_im.reshape(SECTORS, SAMPLES, REC_NODES)
```

```python
import functools
import math

import jax
import jax.numpy as jnp
import numpy as np
from jax import lax
from jax.experimental import pallas as pl
from jax.experimental.pallas import tpu as pltpu
from jax.sharding import PartitionSpec as P

MESH = pl.DeviceIdType.MESH
SECTORS = 64
COLS = 16
LANES = 128
GROUP = 8
CHUNKS = 4
F32 = jnp.float32
BF16 = jnp.bfloat16


def transforms():
    waves = np.arange(SECTORS)
    half = SECTORS // 2
    angle = 2.0 * np.pi / SECTORS * ((waves[:, None] * waves[None, :]) % SECTORS)
    forward = np.concatenate([np.cos(angle[: half + 1]), -np.sin(angle[1:half])], 0)
    weight = np.full((SECTORS,), 2.0 / SECTORS)
    weight[0] = weight[half] = 1.0 / SECTORS
    inverse = forward.T * weight[None, :]
    eye = np.eye(GROUP)
    return (
        np.kron(forward, eye).astype(jnp.bfloat16),
        np.kron(inverse, eye).astype(jnp.bfloat16),
    )


def kernel(
    press_hbm, basis_hbm, rec_hbm, omega_hbm, damp_hbm, harm_hbm, fwd_hbm, inv_hbm,
    out_re, out_im,
    press, basis, rec, omega, damp, harm, fwd, inv,
    own, give, take, params, params_in, recv_re, recv_im,
    ring_out, ring_in, loads_out, loads_in, resp_out, gathered, total,
    stage_re, stage_im,
    load_sem, give_s, give_r, par_sem, ring_s, ring_r, fwd_s, fwd_r, back_s, back_r,
    ag_s, ag_r, pair_s, pair_r, out_sem,
):
    col = lax.axis_index("sector")
    place = lax.axis_index("mode")
    z = place // 2
    core = place % 2
    other = 1 - core
    y = col // 4
    partner = (col, z * 2 + other)

    def at_z(step):
        return (z + step + 8) % 8

    up = (col, at_z(1) * 2 + core)
    down = (col, at_z(-1) * 2 + core)
    beside = (up, down)

    loads = [
        pltpu.make_async_copy(a, b, load_sem.at[n])
        for n, (a, b) in enumerate(
            (
                (press_hbm, press), (basis_hbm, basis), (omega_hbm, omega),
                (damp_hbm, damp), (harm_hbm, harm), (fwd_hbm, fwd), (inv_hbm, inv),
                (rec_hbm, rec),
            )
        )
    ]
    for copy in loads:
        copy.start()

    barrier = pltpu.get_barrier_semaphore()
    for device in (up, down, partner):
        pl.semaphore_signal(barrier, inc=1, device_id=device, device_id_type=MESH)
    for step in range(1, COLS):
        pl.semaphore_signal(
            barrier, inc=1, device_id=((col + step) % COLS, place), device_id_type=MESH
        )

    loads[0].wait()
    loads[1].wait()

    def partial(half, target):
        rows = press[:, pl.ds(pl.multiple_of(half * 128, 128), 128), :].reshape(512, 1024)

        def tile(n, _):
            part = jnp.dot(
                rows,
                basis[:, pl.ds(pl.multiple_of(n * 256, 256), 256)],
                preferred_element_type=F32,
            ).astype(target.dtype)
            for b in range(2):
                for q in range(CHUNKS):
                    for s in range(4):
                        target[2 * n + b, q, s * 32 : s * 32 + 32, :] = part[
                            s * 128 + q * 32 : s * 128 + q * 32 + 32, b * 128 : b * 128 + 128
                        ]
            return 0

        lax.fori_loop(0, 4, tile, 0)

    partial(other, give)
    partial(core, own)

    loads[2].wait()
    loads[3].wait()
    loads[4].wait()
    params[...] = jnp.zeros_like(params)
    for n, ref in enumerate((omega, damp)):
        mine = ref[...]
        none = jnp.zeros_like(mine)
        params[n, 0:33, :] = jnp.concatenate(
            [jnp.where(core == 0, mine, none), jnp.where(core == 1, mine, none)], 1
        )

    pl.semaphore_wait(barrier, COLS + 2)

    def pair_copy(n, block):
        return pltpu.make_async_remote_copy(
            src_ref=give.at[block], dst_ref=take.at[block], send_sem=give_s.at[n],
            recv_sem=give_r.at[n], device_id=partner, device_id_type=MESH,
        )

    order = (4, 3, -3, 2, -2, 1, -1, 0)
    pair_copies = {}
    for n, step in enumerate(order):
        pair_copies[step] = pair_copy(n, at_z(step))
        pair_copies[step].start()
    par_copy = pltpu.make_async_remote_copy(
        src_ref=params, dst_ref=params_in, send_sem=par_sem.at[0], recv_sem=par_sem.at[1],
        device_id=partner, device_id_type=MESH,
    )
    par_copy.start()

    def ring_copy(way, hop, q):
        return pltpu.make_async_remote_copy(
            src_ref=ring_out.at[way, hop, q], dst_ref=ring_in.at[way, hop, q],
            send_sem=ring_s.at[way, hop, q], recv_sem=ring_r.at[way, hop, q],
            device_id=beside[way], device_id_type=MESH,
        )

    def ring_step(way, hop, q, add):
        block = at_z((4 - hop) * (1, -1)[way])
        value = own[block, q] + take[block, q].astype(F32)
        if add:
            ring_copy(way, hop - 1, q).wait_recv()
            value = value + ring_in[way, hop - 1, q].astype(F32)
        ring_out[way, hop, q] = value.astype(BF16)
        ring_copy(way, hop, q).start()

    longer = ((0, 1), (2, 3))
    shorter = ((2, 3), (0, 1))
    pair_copies[4].wait_recv()
    for n in range(2):
        for way in range(2):
            ring_step(way, 0, longer[way][n], False)
    for hop in range(1, 4):
        pair_copies[4 - hop].wait_recv()
        pair_copies[hop - 4].wait_recv()
        for n in range(2):
            for way in range(2):
                ring_step(way, hop, shorter[way][n], hop > 1)
        for n in range(2):
            for way in range(2):
                ring_step(way, hop, longer[way][n], True)
        if hop == 1:
            par_copy.wait_recv()
            both = params[...] + params_in[...]
            freq = both[0, 0:33, :][:, None, :]
            ratio = both[1, 0:33, :][:, None, :]
            sample = lax.broadcasted_iota(jnp.int32, (GROUP, 256), 0)
            lane = lax.broadcasted_iota(jnp.int32, (GROUP, 256), 1)
            here = lane == core * 128 + col * GROUP + sample
            picked = jnp.where(here, harm[...].astype(F32), 0.0)
            drive = (0.25 * jnp.sum(picked, axis=1, keepdims=True))[None, :, :]
            stiff = freq * freq - drive * drive
            loss = 2.0 * ratio * freq * drive
            size = stiff * stiff + loss * loss
            for ref, value in ((recv_re, stiff / size), (recv_im, -loss / size)):
                ref[0:33] = value
                ref[33:64] = value[1:32]

    def fwd_copy(to, source):
        return pltpu.make_async_remote_copy(
            src_ref=loads_out.at[to], dst_ref=loads_in.at[source], send_sem=fwd_s.at[to],
            recv_sem=fwd_r.at[source], device_id=(to, place), device_id_type=MESH,
        )

    pair_copies[0].wait_recv()
    for q in range(CHUNKS):
        for way in range(2):
            ring_copy(way, 3, q).wait_recv()
        force = (
            own[z, q] + take[z, q].astype(F32)
            + ring_in[0, 3, q].astype(F32) + ring_in[1, 3, q].astype(F32)
        )
        for o in range(4):
            to = q * 4 + o
            for pair in range(2):
                at = 2 * pair * 32 + o * 8
                loads_out[to, pair] = jnp.concatenate(
                    [force[at : at + 8], force[at + 32 : at + 40]], 0
                ).astype(BF16)

            @pl.when(to != col)
            def _():
                fwd_copy(to, col).start()

    loads_in[col] = loads_out[col]

    loads[5].wait()
    loads[6].wait()
    for source in range(COLS):

        @pl.when(source != col)
        def _():
            fwd_copy(source, source).wait_recv()

    wave = jnp.dot(fwd[...], loads_in[...].reshape(512, LANES), preferred_element_type=F32)
    response = jnp.concatenate(
        [
            (wave * recv_re[...].reshape(512, LANES)).astype(BF16),
            (wave * recv_im[...].reshape(512, LANES)).astype(BF16),
        ],
        1,
    )
    back = jnp.dot(inv[...], response, preferred_element_type=F32)
    resp_out[...] = jnp.concatenate(
        [
            back[:, :LANES].reshape(SECTORS, GROUP, LANES),
            back[:, LANES:].reshape(SECTORS, GROUP, LANES),
        ],
        1,
    ).astype(BF16)

    def back_copy(to, source):
        return pltpu.make_async_remote_copy(
            src_ref=resp_out.at[pl.ds(to * 4, 4)],
            dst_ref=gathered.at[z, core, source // 4, source % 4],
            send_sem=back_s.at[to], recv_sem=back_r.at[source],
            device_id=(to, place), device_id_type=MESH,
        )

    for step in (10, 9, 11, 6, 14, 5, 7, 13, 15, 2, 8, 1, 3, 4, 12):
        back_copy((col + step) % COLS, col).start()
    gathered[z, core, y, col % 4] = resp_out[pl.ds(col * 4, 4)]

    def ag_copy(way, hop, q):
        block = at_z((1 - hop) * (1, -1)[way])
        return pltpu.make_async_remote_copy(
            src_ref=gathered.at[block, core, q], dst_ref=gathered.at[block, core, q],
            send_sem=ag_s.at[way, hop - 1, q], recv_sem=ag_r.at[way, hop - 1, q],
            device_id=beside[way], device_id_type=MESH,
        )

    def ag_arrival(way, hop, q):
        block = at_z(hop * (-1, 1)[way])
        return pltpu.make_async_remote_copy(
            src_ref=gathered.at[block, core, q], dst_ref=gathered.at[block, core, q],
            send_sem=ag_s.at[way, hop - 1, q], recv_sem=ag_r.at[way, hop - 1, q],
            device_id=beside[way], device_id_type=MESH,
        )

    def share(step, q, half):
        block = at_z(step)
        return pltpu.make_async_remote_copy(
            src_ref=gathered.at[block, half, q], dst_ref=gathered.at[block, half, q],
            send_sem=pair_s.at[step + 3, q], recv_sem=pair_r.at[step + 3, q],
            device_id=partner, device_id_type=MESH,
        )

    loads[7].wait()

    def product(one, two, half, q):
        left = jnp.concatenate(
            [
                gathered[at_z(one), half, q].reshape(256, LANES),
                gathered[at_z(two), half, q].reshape(256, LANES),
            ],
            1,
        )
        right = jnp.concatenate([rec[at_z(one)], rec[at_z(two)]], 0)
        return jnp.dot(left, right, preferred_element_type=F32)

    def out_copies(half, q):
        rows = pl.ds(pl.multiple_of(half * 128 + q * 32, 32), 32)
        return [
            pltpu.make_async_copy(
                stage.at[:, rows, :], out.at[:, rows, :], out_sem.at[n, half, q]
            )
            for n, (stage, out) in enumerate(((stage_re, out_re), (stage_im, out_im)))
        ]

    def task(hop, half, q):
        if hop == 1:
            total[half, q] = product(-1, 1, half, q)
        elif hop < 4:
            total[half, q] += product(-hop, hop, half, q)
        else:
            stress = total[half, q] + product(0, 4, half, q)
            rows = pl.ds(pl.multiple_of(half * 128 + q * 32, 32), 32)
            for s in range(4):
                for n, stage in enumerate((stage_re, stage_im)):
                    stage[s, rows, :] = jnp.concatenate(
                        [stress[o * 64 + s * 16 + n * 8 :][:8] for o in range(4)], 0
                    ).astype(BF16)
            for copy in out_copies(half, q):
                copy.start()

    for q in range(CHUNKS):
        for o in range(4):
            source = q * 4 + o

            @pl.when(source != col)
            def _():
                back_copy(source, source).wait_recv()

        ag_copy(0, 1, q).start()
        ag_copy(1, 1, q).start()
        share(0, q, core).start()

    def shared_wait(hop, q):
        if hop < 4:
            share(-hop, q, other).wait_recv()
            share(hop, q, other).wait_recv()
        else:
            share(0, q, other).wait_recv()
            share(4, q, other).wait_recv()

    for hop in range(1, 4):

        def step(q, _, hop=hop, ways=(0, 1)):
            for way in range(2):
                ag_arrival(way, hop, q).wait_recv()
                if way in ways:
                    ag_copy(way, hop + 1, q).start()
                share(hop * (-1, 1)[way], q, core).start()
            task(hop, core, q)
            if hop > 1:
                shared_wait(hop - 1, q)
                task(hop - 1, other, q)
            return 0

        if hop < 3:
            lax.fori_loop(0, CHUNKS, step, 0)
        else:
            lax.fori_loop(0, 2, functools.partial(step, ways=(0,)), 0)
            lax.fori_loop(2, 4, functools.partial(step, ways=(1,)), 0)

    for way in range(2):

        def last(q, _, way=way):
            ag_arrival(way, 4, q).wait_recv()
            share(4, q, core).start()
            task(4, core, q)
            shared_wait(3, q)
            task(3, other, q)
            return 0

        lax.fori_loop(2 * way, 2 * way + 2, last, 0)

    def finish(q, _):
        shared_wait(4, q)
        task(4, other, q)
        return 0

    lax.fori_loop(0, CHUNKS, finish, 0)

    for copy in pair_copies.values():
        copy.wait_send()
    par_copy.wait_send()
    for way in range(2):
        for q in range(CHUNKS):
            for hop in range(4):
                if hop > 0 or q in longer[way]:
                    ring_copy(way, hop, q).wait_send()
                if hop < 3 or q in longer[way]:
                    ag_copy(way, hop + 1, q).wait_send()
    for n in range(COLS):

        @pl.when(n != col)
        def _():
            fwd_copy(n, col).wait_send()
            back_copy(n, col).wait_send()

    def ends(q, _):
        for step in range(-3, 5):
            share(step, q, core).wait_send()
        for half in range(2):
            for copy in out_copies(half, q):
                copy.wait()
        return 0

    lax.fori_loop(0, CHUNKS, ends, 0)


def local(pressure, basis, recovery, omega, damping, harmonic):
    fwd, inv = transforms()
    dma = pltpu.SemaphoreType.DMA
    anywhere = pl.BlockSpec(memory_space=pl.ANY)
    out = jax.ShapeDtypeStruct((4, 256, 1024), BF16)
    return pl.pallas_call(
        kernel,
        out_shape=(out, out),
        in_specs=[anywhere] * 8,
        out_specs=(anywhere, anywhere),
        scratch_shapes=[
            pltpu.VMEM((4, 256, 1024), BF16),
            pltpu.VMEM((1024, 1024), BF16),
            pltpu.VMEM((8, 128, 1024), BF16),
            pltpu.VMEM((33, 64), F32),
            pltpu.VMEM((33, 64), F32),
            pltpu.VMEM((1, 256), jnp.int32),
            pltpu.VMEM((512, 512), BF16),
            pltpu.VMEM((512, 512), BF16),
            pltpu.VMEM((8, CHUNKS, 128, LANES), F32),
            pltpu.VMEM((8, CHUNKS, 128, LANES), BF16),
            pltpu.VMEM((8, CHUNKS, 128, LANES), BF16),
            pltpu.VMEM((2, 40, LANES), F32),
            pltpu.VMEM((2, 40, LANES), F32),
            pltpu.VMEM((SECTORS, GROUP, LANES), F32),
            pltpu.VMEM((SECTORS, GROUP, LANES), F32),
            pltpu.VMEM((2, 4, CHUNKS, 128, LANES), BF16),
            pltpu.VMEM((2, 4, CHUNKS, 128, LANES), BF16),
            pltpu.VMEM((COLS, 2, 16, LANES), BF16),
            pltpu.VMEM((COLS, 2, 16, LANES), BF16),
            pltpu.VMEM((SECTORS, 16, LANES), BF16),
            pltpu.VMEM((8, 2, CHUNKS, 4, 4, 16, LANES), BF16),
            pltpu.VMEM((2, CHUNKS, 256, 1024), F32),
            pltpu.VMEM((4, 256, 1024), BF16),
            pltpu.VMEM((4, 256, 1024), BF16),
            dma((8,)),
            dma((8,)), dma((8,)),
            dma((2,)),
            dma((2, 4, CHUNKS)), dma((2, 4, CHUNKS)),
            dma((COLS,)), dma((COLS,)),
            dma((COLS,)), dma((COLS,)),
            dma((2, 4, CHUNKS)), dma((2, 4, CHUNKS)),
            dma((8, CHUNKS)), dma((8, CHUNKS)),
            dma((2, 2, CHUNKS)),
        ],
        compiler_params=pltpu.CompilerParams(
            collective_id=0, has_side_effects=True, vmem_limit_bytes=52 * 2**20
        ),
        cost_estimate=pl.CostEstimate(
            flops=7 * 2**30, bytes_accessed=12 * 2**20, transcendentals=0
        ),
    )(
        pressure, basis, recovery.reshape(8, 128, 1024), omega, damping,
        harmonic.reshape(1, 256), fwd, inv,
    )


def solution(mesh):
    in_specs = (
        P("sector", None, "mode"),
        P("mode", None),
        P(None, "mode"),
        P(None, "mode"),
        P(None, "mode"),
        P(),
    )
    out_specs = (P("sector", None, "mode"), P("sector", None, "mode"))
    return jax.shard_map(local, mesh=mesh, in_specs=in_specs, out_specs=out_specs, check_vma=False)
```

```python
import functools
import math

import jax
import jax.numpy as jnp
from jax import lax
from jax.experimental import pallas as pl
from jax.experimental.pallas import tpu as pltpu
from jax.sharding import PartitionSpec as P

MESH = pl.DeviceIdType.MESH
SECTORS = 64
COLS = 16
LANES = 128
GROUP = 8
CHUNKS = 4
DIRECT = 2
F32 = jnp.float32
BF16 = jnp.bfloat16


def phase_values(diameter_dim):
    shape = (SECTORS, SECTORS)
    number = lax.broadcasted_iota(jnp.int32, shape, diameter_dim)
    sector = lax.broadcasted_iota(jnp.int32, shape, 1 - diameter_dim)
    half = SECTORS // 2
    sine = number > half
    diameter = jnp.where(sine, number - half, number)
    angle = (2.0 * math.pi / SECTORS) * ((diameter * sector) % SECTORS).astype(F32)
    value = jnp.where(sine, -jnp.sin(angle), jnp.cos(angle))
    once = (number == 0) | (number == half)
    return value, jnp.where(once, 1.0 / SECTORS, 2.0 / SECTORS)


def per_sample(table):
    size = SECTORS * GROUP
    rows = jnp.broadcast_to(table[:, None, :], (SECTORS, GROUP, SECTORS)).reshape(size, SECTORS)
    spread = (
        lax.broadcasted_iota(jnp.int32, (SECTORS, size), 0)
        == lax.broadcasted_iota(jnp.int32, (SECTORS, size), 1) // GROUP
    )
    wide = jnp.dot(
        rows.astype(BF16), spread.astype(F32).astype(BF16), preferred_element_type=F32
    )
    same = (
        lax.broadcasted_iota(jnp.int32, (size, size), 0) % GROUP
        == lax.broadcasted_iota(jnp.int32, (size, size), 1) % GROUP
    )
    return jnp.where(same, wide, 0.0).astype(BF16)


def kernel(
    press_hbm, basis_hbm, rec_hbm, omega_hbm, damp_hbm, harm_hbm,
    stage_re, stage_im,
    press, basis, rec, omega, damp, harm, fwd, inv,
    own, give, take, params, params_in, recv_re, recv_im,
    ring_out, ring_in, loads_out, loads_in, resp_out, gathered, total,
    load_sem, give_s, give_r, par_sem, ring_s, ring_r, fwd_s, fwd_r, back_s, back_r,
    ag_s, ag_r, pair_s, pair_r, ready,
):
    col = lax.axis_index("sector")
    place = lax.axis_index("mode")
    z = place // 2
    core = place % 2
    other = 1 - core
    y = col // 4
    partner = (col, z * 2 + other)

    def at_z(step):
        return (z + step + 8) % 8

    up = (col, at_z(1) * 2 + core)
    down = (col, at_z(-1) * 2 + core)
    beside = (up, down)

    def samples(half):
        return pl.ds(pl.multiple_of(half * 128, 128), 128)

    load_press = [
        pltpu.make_async_copy(
            press_hbm.at[:, samples(half), :], press.at[:, samples(half), :], load_sem.at[n]
        )
        for n, half in enumerate((other, core))
    ]
    def load_basis(n):
        columns = pl.ds(n * 256 if isinstance(n, int) else pl.multiple_of(n * 256, 256), 256)
        return pltpu.make_async_copy(
            basis_hbm.at[:, columns], basis.at[:, columns], load_sem.at[2 + n]
        )

    load_small = [
        pltpu.make_async_copy(a, b, load_sem.at[6 + n])
        for n, (a, b) in enumerate(((omega_hbm, omega), (damp_hbm, damp), (harm_hbm, harm)))
    ]
    load_rec = pltpu.make_async_copy(rec_hbm, rec, load_sem.at[9])
    load_press[0].start()
    for n in range(4):
        load_basis(n).start()
    load_press[1].start()
    for copy in load_small:
        copy.start()

    barrier = pltpu.get_barrier_semaphore()
    for device in (up, down, partner):
        pl.semaphore_signal(barrier, inc=1, device_id=device, device_id_type=MESH)
    for step in range(1, COLS):
        pl.semaphore_signal(
            barrier, inc=1, device_id=((col + step) % COLS, place), device_id_type=MESH
        )

    def partial(half, target, n):
        part = jnp.dot(
            press[:, samples(half), :].reshape(512, 1024),
            basis[:, pl.ds(pl.multiple_of(n * 256, 256), 256)],
            preferred_element_type=F32,
        ).astype(target.dtype)
        for b in range(2):
            for q in range(CHUNKS):
                for s in range(4):
                    target[2 * n + b, q, s * 32 : s * 32 + 32, :] = part[
                        s * 128 + q * 32 : s * 128 + q * 32 + 32, b * 128 : b * 128 + 128
                    ]

    def give_tile(n, _):
        load_basis(n).wait()
        partial(other, give, n)
        return 0

    def own_tile(n, _):
        partial(core, own, (z // 2 + 2 + n) % 4)
        return 0

    load_press[0].wait()
    lax.fori_loop(0, 4, give_tile, 0)
    load_press[1].wait()
    pl.semaphore_wait(barrier, COLS + 2)

    def pair_copy(n, block):
        return pltpu.make_async_remote_copy(
            src_ref=give.at[block], dst_ref=take.at[block], send_sem=give_s.at[n],
            recv_sem=give_r.at[n], device_id=partner, device_id_type=MESH,
        )

    order = (4, 3, -3, 2, -2, 1, -1, 0)
    pair_copies = {}
    for n, step in enumerate(order):
        pair_copies[step] = pair_copy(n, at_z(step))
        pair_copies[step].start()
    for step in range(1, COLS):
        pl.semaphore_signal(
            ready, inc=1, device_id=((col + step) % COLS, place), device_id_type=MESH
        )
    load_rec.start()

    longer = ((0, 2), (1, 3))
    shorter = ((1, 3), (0, 2))

    def ring_copy(way, hop, q):
        return pltpu.make_async_remote_copy(
            src_ref=ring_out.at[way, hop, q], dst_ref=ring_in.at[way, hop, q],
            send_sem=ring_s.at[way, hop, q], recv_sem=ring_r.at[way, hop, q],
            device_id=beside[way], device_id_type=MESH,
        )

    def pair_sum(block, q):
        return own[block, q] + take[block, q].astype(F32)

    def ring_sum(way, hop, q):
        value = pair_sum(at_z((4 - hop) * (1, -1)[way]), q)
        if hop > 1 or (hop == 1 and q in longer[way]):
            ring_copy(way, hop - 1, q).wait_recv()
            value = value + ring_in[way, hop - 1, q].astype(F32)
        return value

    def ring_steps(hop, chunks):
        for n in range(2):
            for way in range(2):
                q = chunks[way][n]
                ring_out[way, hop, q] = ring_sum(way, hop, q).astype(BF16)
                ring_copy(way, hop, q).start()

    planes = (place, at_z(1) * 2 + core, at_z(-1) * 2 + core)

    def fwd_copy(kind, to, source):
        return pltpu.make_async_remote_copy(
            src_ref=loads_out.at[kind, to], dst_ref=loads_in.at[kind, source],
            send_sem=fwd_s.at[kind, to], recv_sem=fwd_r.at[kind, source],
            device_id=(to, planes[kind]), device_id_type=MESH,
        )

    def send_loads(kind, q, force):
        for o in range(4):
            to = q * 4 + o
            for pair in range(2):
                at = 2 * pair * 32 + o * 8
                loads_out[kind, to, pair] = jnp.concatenate(
                    [force[at : at + 8], force[at + 32 : at + 40]], 0
                ).astype(BF16)
            if kind:
                fwd_copy(kind, to, col).start()
            else:

                @pl.when(to != col)
                def _():
                    fwd_copy(0, to, col).start()

                @pl.when(to == col)
                def _():
                    loads_in[0, col] = loads_out[0, col]

    lax.fori_loop(0, 1, own_tile, 0)
    pair_copies[4].wait_recv()
    ring_steps(0, longer)
    lax.fori_loop(1, 4, own_tile, 0)
    for step in (3, -3):
        pair_copies[step].wait_recv()
    ring_steps(1, shorter)
    for step in (2, -2, 1, -1, 0):
        pair_copies[step].wait_recv()
    for q in range(CHUNKS):
        send_loads(0, q, pair_sum(z, q))

    for copy in load_small:
        copy.wait()
    params[...] = jnp.zeros_like(params)
    for n, ref in enumerate((omega, damp)):
        mine = ref[...]
        none = jnp.zeros_like(mine)
        params[n, 0:33, :] = jnp.concatenate(
            [jnp.where(core == 0, mine, none), jnp.where(core == 1, mine, none)], 1
        )

    par_copy = pltpu.make_async_remote_copy(
        src_ref=params, dst_ref=params_in, send_sem=par_sem.at[0], recv_sem=par_sem.at[1],
        device_id=partner, device_id_type=MESH,
    )
    par_copy.start()

    ring_steps(1, longer)

    forward, _ = phase_values(0)
    fwd[...] = per_sample(forward)
    backward, weight = phase_values(1)
    inv[...] = per_sample(backward * weight)

    ring_steps(2, shorter)
    ring_steps(2, longer)

    par_copy.wait_recv()
    both = params[...] + params_in[...]
    freq = both[0, 0:33, :][:, None, :]
    ratio = both[1, 0:33, :][:, None, :]
    sample = lax.broadcasted_iota(jnp.int32, (GROUP, 256), 0)
    lane = lax.broadcasted_iota(jnp.int32, (GROUP, 256), 1)
    here = lane == core * 128 + col * GROUP + sample
    picked = jnp.where(here, harm[...].astype(F32), 0.0)
    drive = (0.25 * jnp.sum(picked, axis=1, keepdims=True))[None, :, :]
    stiff = freq * freq - drive * drive
    loss = 2.0 * ratio * freq * drive
    size = stiff * stiff + loss * loss
    for ref, value in ((recv_re, stiff / size), (recv_im, -loss / size)):
        ref[0:33] = value
        ref[33:64] = value[1:32]

    pl.semaphore_wait(ready, COLS - 1)
    for chunks in (shorter, longer):
        for n in range(2):
            for way in range(2):
                q = chunks[way][n]
                send_loads(way + 1, q, ring_sum(way, 3, q))

    for source in range(COLS):
        fwd_copy(1, source, source).wait_recv()
        fwd_copy(2, source, source).wait_recv()

        @pl.when(source != col)
        def _():
            fwd_copy(0, source, source).wait_recv()

    force = (
        loads_in[0].astype(F32) + loads_in[1].astype(F32) + loads_in[2].astype(F32)
    ).astype(BF16).reshape(512, LANES)
    wave = jnp.dot(fwd[...], force, preferred_element_type=F32)
    response = jnp.concatenate(
        [
            (wave * recv_re[...].reshape(512, LANES)).astype(BF16),
            (wave * recv_im[...].reshape(512, LANES)).astype(BF16),
        ],
        1,
    )
    back = jnp.dot(inv[...], response, preferred_element_type=F32)
    resp_out[...] = jnp.concatenate(
        [
            back[:, :LANES].reshape(SECTORS, GROUP, LANES),
            back[:, LANES:].reshape(SECTORS, GROUP, LANES),
        ],
        1,
    ).astype(BF16)

    def back_copy(kind, to, source):
        return pltpu.make_async_remote_copy(
            src_ref=resp_out.at[pl.ds(to * 4, 4)],
            dst_ref=gathered.at[z, core, source // 4, source % 4],
            send_sem=back_s.at[kind, to], recv_sem=back_r.at[kind, source],
            device_id=(to, planes[kind]), device_id_type=MESH,
        )

    for step in (10, 9, 11, 6, 14, 5, 7, 13, 15, 2, 8, 1, 3, 4, 12, 0):
        to = (col + step) % COLS

        @pl.when(y < DIRECT)
        def _():
            back_copy(1, to, col).start()
            back_copy(2, to, col).start()

        if step:
            back_copy(0, to, col).start()
    gathered[z, core, y, col % 4] = resp_out[pl.ds(col * 4, 4)]

    def back_arrival(kind, source):
        block = at_z((0, -1, 1)[kind])
        return pltpu.make_async_remote_copy(
            src_ref=resp_out.at[pl.ds(source * 4, 4)],
            dst_ref=gathered.at[block, core, source // 4, source % 4],
            send_sem=back_s.at[kind, source], recv_sem=back_r.at[kind, source],
            device_id=(source, planes[kind]), device_id_type=MESH,
        )

    def ag_copy(way, hop, q):
        block = at_z((1 - hop) * (1, -1)[way])
        return pltpu.make_async_remote_copy(
            src_ref=gathered.at[block, core, q], dst_ref=gathered.at[block, core, q],
            send_sem=ag_s.at[way, hop - 1, q], recv_sem=ag_r.at[way, hop - 1, q],
            device_id=beside[way], device_id_type=MESH,
        )

    def ag_arrival(way, hop, q):
        block = at_z(hop * (-1, 1)[way])
        return pltpu.make_async_remote_copy(
            src_ref=gathered.at[block, core, q], dst_ref=gathered.at[block, core, q],
            send_sem=ag_s.at[way, hop - 1, q], recv_sem=ag_r.at[way, hop - 1, q],
            device_id=beside[way], device_id_type=MESH,
        )

    def share(step, q, half):
        block = at_z(step)
        return pltpu.make_async_remote_copy(
            src_ref=gathered.at[block, half, q], dst_ref=gathered.at[block, half, q],
            send_sem=pair_s.at[step + 3, q], recv_sem=pair_r.at[step + 3, q],
            device_id=partner, device_id_type=MESH,
        )

    load_rec.wait()

    def task(hop, half, q):
        one, two = (at_z(-hop), at_z(hop)) if hop < 4 else (at_z(0), at_z(4))
        rows = pl.ds(pl.multiple_of(half * 128 + q * 32, 32), 32)

        left = jnp.concatenate([gathered[b, half, q].reshape(256, LANES) for b in (one, two)], 1)
        right = jnp.concatenate([rec[b] for b in (one, two)], 0)
        part = jnp.dot(left, right, preferred_element_type=F32)
        if hop == 1:
            total[half, q] = part
        elif hop < 4:
            total[half, q] += part
        else:
            stress = total[half, q] + part
            for s in range(4):
                for n, stage in enumerate((stage_re, stage_im)):
                    stage[s, rows, :] = jnp.concatenate(
                        [stress[o * 64 + s * 16 + n * 8 :][:8] for o in range(4)], 0
                    ).astype(BF16)

    def begin(q):
        for o in range(4):
            source = q * 4 + o

            @pl.when(source != col)
            def _():
                back_arrival(0, source).wait_recv()

        if q >= DIRECT:
            ag_copy(0, 1, q).start()
            ag_copy(1, 1, q).start()
        share(0, q, core).start()

    def arrive(hop, q):
        for way in range(2):
            if hop < 4 or q in longer[way]:
                if hop == 1 and q < DIRECT:
                    for o in range(4):
                        back_arrival(way + 1, q * 4 + o).wait_recv()
                else:
                    ag_arrival(way, hop, q).wait_recv()
                if hop < 3 or (hop == 3 and q in longer[way]):
                    ag_copy(way, hop + 1, q).start()
                share(hop * (-1, 1)[way] if hop < 4 else 4, q, core).start()

    def shared_task(hop, q):
        for step in (-hop, hop) if hop < 4 else (0, 4):
            share(step, q, other).wait_recv()
        task(hop, other, q)

    begin(2)
    begin(3)
    pending = None
    for hop, q in (
        (1, 0), (1, 1), (0, 0), (0, 1), (1, 2), (1, 3), (2, 0), (2, 1), (2, 2), (2, 3),
        (3, 0), (3, 1), (3, 2), (3, 3), (4, 0), (4, 1), (4, 2), (4, 3),
    ):
        if hop == 0:
            begin(q)
            continue
        arrive(hop, q)
        task(hop, core, q)
        if pending is not None:
            shared_task(*pending)
        pending = (hop, q)
    shared_task(*pending)

    for copy in pair_copies.values():
        copy.wait_send()
    par_copy.wait_send()
    for way in range(2):
        for q in range(CHUNKS):
            for hop in range(4):
                if hop < 3 and (hop > 0 or q in longer[way]):
                    ring_copy(way, hop, q).wait_send()
                if (hop > 0 or q >= DIRECT) and (hop < 3 or q in longer[way]):
                    ag_copy(way, hop + 1, q).wait_send()
    for n in range(COLS):
        for kind in (1, 2):
            fwd_copy(kind, n, col).wait_send()

            @pl.when(y < DIRECT)
            def _():
                back_copy(kind, n, col).wait_send()

        @pl.when(n != col)
        def _():
            fwd_copy(0, n, col).wait_send()
            back_copy(0, n, col).wait_send()

    def ends(q, _):
        for step in range(-3, 5):
            share(step, q, core).wait_send()
        return 0

    lax.fori_loop(0, CHUNKS, ends, 0)


def write_out(stage_re, stage_im, out_re, out_im, sem):
    copies = [
        pltpu.make_async_copy(stage.at[s], out.at[s], sem.at[n, s])
        for n, (stage, out) in enumerate(((stage_re, out_re), (stage_im, out_im)))
        for s in range(4)
    ]
    for copy in copies:
        copy.start()
    for copy in copies:
        copy.wait()


def local(pressure, basis, recovery, omega, damping, harmonic):
    dma = pltpu.SemaphoreType.DMA
    anywhere = pl.BlockSpec(memory_space=pl.ANY)
    held = pl.BlockSpec(memory_space=pltpu.VMEM)
    out = jax.ShapeDtypeStruct((4, 256, 1024), BF16)
    stage = pltpu.VMEM((4, 256, 1024), BF16)
    staged = pl.pallas_call(
        kernel,
        out_shape=(stage, stage),
        in_specs=[anywhere] * 6,
        out_specs=(held, held),
        scratch_shapes=[
            pltpu.VMEM((4, 256, 1024), BF16),
            pltpu.VMEM((1024, 1024), BF16),
            pltpu.VMEM((8, 128, 1024), BF16),
            pltpu.VMEM((33, 64), F32),
            pltpu.VMEM((33, 64), F32),
            pltpu.VMEM((1, 256), jnp.int32),
            pltpu.VMEM((512, 512), BF16),
            pltpu.VMEM((512, 512), BF16),
            pltpu.VMEM((8, CHUNKS, 128, LANES), F32),
            pltpu.VMEM((8, CHUNKS, 128, LANES), BF16),
            pltpu.VMEM((8, CHUNKS, 128, LANES), BF16),
            pltpu.VMEM((2, 40, LANES), F32),
            pltpu.VMEM((2, 40, LANES), F32),
            pltpu.VMEM((SECTORS, GROUP, LANES), F32),
            pltpu.VMEM((SECTORS, GROUP, LANES), F32),
            pltpu.VMEM((2, 4, CHUNKS, 128, LANES), BF16),
            pltpu.VMEM((2, 4, CHUNKS, 128, LANES), BF16),
            pltpu.VMEM((3, COLS, 2, 16, LANES), BF16),
            pltpu.VMEM((3, COLS, 2, 16, LANES), BF16),
            pltpu.VMEM((SECTORS, 16, LANES), BF16),
            pltpu.VMEM((8, 2, CHUNKS, 4, 4, 16, LANES), BF16),
            pltpu.VMEM((2, CHUNKS, 256, 1024), F32),
            dma((10,)),
            dma((8,)), dma((8,)),
            dma((2,)),
            dma((2, 4, CHUNKS)), dma((2, 4, CHUNKS)),
            dma((3, COLS)), dma((3, COLS)),
            dma((3, COLS)), dma((3, COLS)),
            dma((2, 4, CHUNKS)), dma((2, 4, CHUNKS)),
            dma((8, CHUNKS)), dma((8, CHUNKS)),
            pltpu.SemaphoreType.REGULAR,
        ],
        compiler_params=pltpu.CompilerParams(
            collective_id=0, has_side_effects=True, vmem_limit_bytes=52 * 2**20
        ),
        cost_estimate=pl.CostEstimate(
            flops=7 * 2**30, bytes_accessed=12 * 2**20, transcendentals=0
        ),
    )(
        *(
            pltpu.with_memory_space_constraint(array, pltpu.HBM)
            for array in (
                pressure, basis, recovery.reshape(8, 128, 1024), omega, damping,
                harmonic.reshape(1, 256),
            )
        )
    )
    return pl.pallas_call(
        write_out,
        out_shape=(out, out),
        in_specs=[anywhere, anywhere],
        out_specs=(anywhere, anywhere),
        scratch_shapes=[dma((2, 4))],
        compiler_params=pltpu.CompilerParams(vmem_limit_bytes=2**20),
    )(*(pltpu.with_memory_space_constraint(array, pltpu.VMEM) for array in staged))


def solution(mesh):
    in_specs = (
        P("sector", None, "mode"),
        P("mode", None),
        P(None, "mode"),
        P(None, "mode"),
        P(None, "mode"),
        P(),
    )
    out_specs = (P("sector", None, "mode"), P("sector", None, "mode"))
    return jax.shard_map(local, mesh=mesh, in_specs=in_specs, out_specs=out_specs, check_vma=False)
```

```python
import functools
import math

import jax
import jax.numpy as jnp
from jax import lax
from jax.experimental import pallas as pl
from jax.experimental.pallas import tpu as pltpu
from jax.sharding import PartitionSpec as P

MESH = pl.DeviceIdType.MESH
SECTORS = 64
COLS = 16
LANES = 128
GROUP = 8
CHUNKS = 4
DIRECT = 2
F32 = jnp.float32
BF16 = jnp.bfloat16


def phase_values(diameter_dim):
    shape = (SECTORS, SECTORS)
    number = lax.broadcasted_iota(jnp.int32, shape, diameter_dim)
    sector = lax.broadcasted_iota(jnp.int32, shape, 1 - diameter_dim)
    half = SECTORS // 2
    sine = number > half
    diameter = jnp.where(sine, number - half, number)
    angle = (2.0 * math.pi / SECTORS) * ((diameter * sector) % SECTORS).astype(F32)
    value = jnp.where(sine, -jnp.sin(angle), jnp.cos(angle))
    once = (number == 0) | (number == half)
    return value, jnp.where(once, 1.0 / SECTORS, 2.0 / SECTORS)


def per_sample(table):
    size = SECTORS * GROUP
    rows = jnp.broadcast_to(table[:, None, :], (SECTORS, GROUP, SECTORS)).reshape(size, SECTORS)
    spread = (
        lax.broadcasted_iota(jnp.int32, (SECTORS, size), 0)
        == lax.broadcasted_iota(jnp.int32, (SECTORS, size), 1) // GROUP
    )
    wide = jnp.dot(
        rows.astype(BF16), spread.astype(F32).astype(BF16), preferred_element_type=F32
    )
    same = (
        lax.broadcasted_iota(jnp.int32, (size, size), 0) % GROUP
        == lax.broadcasted_iota(jnp.int32, (size, size), 1) % GROUP
    )
    return jnp.where(same, wide, 0.0).astype(BF16)


def kernel(
    press_hbm, basis_hbm, rec_hbm, omega_hbm, damp_hbm, harm_hbm,
    stage_re, stage_im,
    press, basis, rec, omega, damp, harm, fwd, inv,
    own, give, take, params, params_in, recv_re, recv_im,
    ring_out, ring_in, loads_out, loads_in, resp_out, gathered, total,
    load_sem, give_s, give_r, par_sem, ring_s, ring_r, fwd_s, fwd_r, back_s, back_r,
    ag_s, ag_r, pair_s, pair_r, ready,
):
    col = lax.axis_index("sector")
    place = lax.axis_index("mode")
    z = place // 2
    core = place % 2
    other = 1 - core
    y = col // 4
    partner = (col, z * 2 + other)

    def at_z(step):
        return (z + step + 8) % 8

    up = (col, at_z(1) * 2 + core)
    down = (col, at_z(-1) * 2 + core)
    beside = (up, down)

    def samples(half):
        return pl.ds(pl.multiple_of(half * 128, 128), 128)

    load_press = [
        pltpu.make_async_copy(
            press_hbm.at[:, samples(half), :], press.at[:, samples(half), :], load_sem.at[n]
        )
        for n, half in enumerate((other, core))
    ]
    def load_basis(n):
        columns = pl.ds(n * 256 if isinstance(n, int) else pl.multiple_of(n * 256, 256), 256)
        return pltpu.make_async_copy(
            basis_hbm.at[:, columns], basis.at[:, columns], load_sem.at[2 + n]
        )

    load_small = [
        pltpu.make_async_copy(a, b, load_sem.at[6 + n])
        for n, (a, b) in enumerate(((omega_hbm, omega), (damp_hbm, damp), (harm_hbm, harm)))
    ]
    load_rec = pltpu.make_async_copy(rec_hbm, rec, load_sem.at[9])
    load_press[0].start()
    for n in range(4):
        load_basis(n).start()
    load_press[1].start()
    for copy in load_small:
        copy.start()

    barrier = pltpu.get_barrier_semaphore()
    for device in (up, down, partner):
        pl.semaphore_signal(barrier, inc=1, device_id=device, device_id_type=MESH)
    for step in range(1, COLS):
        pl.semaphore_signal(
            barrier, inc=1, device_id=((col + step) % COLS, place), device_id_type=MESH
        )

    def partial(half, target, n):
        part = jnp.dot(
            press[:, samples(half), :].reshape(512, 1024),
            basis[:, pl.ds(pl.multiple_of(n * 256, 256), 256)],
            preferred_element_type=F32,
        ).astype(target.dtype)
        for b in range(2):
            for q in range(CHUNKS):
                for s in range(4):
                    target[2 * n + b, q, s * 32 : s * 32 + 32, :] = part[
                        s * 128 + q * 32 : s * 128 + q * 32 + 32, b * 128 : b * 128 + 128
                    ]

    def give_tile(n, _):
        load_basis(n).wait()
        partial(other, give, n)
        return 0

    def own_tile(n, _):
        partial(core, own, (z // 2 + 2 + n) % 4)
        return 0

    load_press[0].wait()
    lax.fori_loop(0, 4, give_tile, 0)
    load_press[1].wait()
    pl.semaphore_wait(barrier, COLS + 2)

    def all_sent(ref, sem):
        pltpu.make_async_remote_copy(
            src_ref=ref, dst_ref=ref, send_sem=sem, recv_sem=sem,
            device_id=partner, device_id_type=MESH,
        ).wait_send()

    def all_arrived(ref, sem):
        pltpu.make_async_remote_copy(
            src_ref=ref, dst_ref=ref, send_sem=sem, recv_sem=sem,
            device_id=partner, device_id_type=MESH,
        ).wait_recv()

    def pair_copy(n, block):
        return pltpu.make_async_remote_copy(
            src_ref=give.at[block], dst_ref=take.at[block], send_sem=give_s.at[0],
            recv_sem=give_r.at[n], device_id=partner, device_id_type=MESH,
        )

    order = (4, 3, -3, 2, -2, 1, -1, 0)
    pair_copies = {}
    for n, step in enumerate(order):
        pair_copies[step] = pair_copy(n, at_z(step))
        pair_copies[step].start()
    for step in range(1, COLS):
        pl.semaphore_signal(
            ready, inc=1, device_id=((col + step) % COLS, place), device_id_type=MESH
        )
    load_rec.start()

    longer = ((0, 2), (1, 3))
    shorter = ((1, 3), (0, 2))

    def ring_slot(way, hop, q):
        return way * 10 + (longer[way].index(q) if hop == 0 else hop * 4 - 2 + q)

    def ring_copy(way, hop, q):
        slot = ring_slot(way, hop, q)
        return pltpu.make_async_remote_copy(
            src_ref=ring_out.at[slot], dst_ref=ring_in.at[slot],
            send_sem=ring_s.at[0], recv_sem=ring_r.at[slot],
            device_id=beside[way], device_id_type=MESH,
        )

    def pair_sum(block, q):
        return own[block, q] + take[block, q].astype(F32)

    def ring_sum(way, hop, q):
        value = pair_sum(at_z((4 - hop) * (1, -1)[way]), q)
        if hop > 1 or (hop == 1 and q in longer[way]):
            ring_copy(way, hop - 1, q).wait_recv()
            value = value + ring_in[ring_slot(way, hop - 1, q)].astype(F32)
        return value

    def ring_steps(hop, chunks):
        for n in range(2):
            for way in range(2):
                q = chunks[way][n]
                ring_out[ring_slot(way, hop, q)] = ring_sum(way, hop, q).astype(BF16)
                ring_copy(way, hop, q).start()

    planes = (place, at_z(1) * 2 + core, at_z(-1) * 2 + core)

    def fwd_copy(kind, to, source):
        return pltpu.make_async_remote_copy(
            src_ref=loads_out.at[kind, to], dst_ref=loads_in.at[kind, source],
            send_sem=fwd_s.at[kind], recv_sem=fwd_r.at[kind],
            device_id=(to, planes[kind]), device_id_type=MESH,
        )

    def send_loads(kind, q, force):
        for o in range(4):
            to = q * 4 + o
            for pair in range(2):
                at = 2 * pair * 32 + o * 8
                loads_out[kind, to, pair] = jnp.concatenate(
                    [force[at : at + 8], force[at + 32 : at + 40]], 0
                ).astype(BF16)
            if kind:
                fwd_copy(kind, to, col).start()
            else:

                @pl.when(to != col)
                def _():
                    fwd_copy(0, to, col).start()

                @pl.when(to == col)
                def _():
                    loads_in[0, col] = loads_out[0, col]

    lax.fori_loop(0, 1, own_tile, 0)
    pair_copies[4].wait_recv()
    ring_steps(0, longer)
    lax.fori_loop(1, 4, own_tile, 0)
    for step in (3, -3):
        pair_copies[step].wait_recv()
    ring_steps(1, shorter)
    for step in (2, -2, 1, -1, 0):
        pair_copies[step].wait_recv()
    for q in range(CHUNKS):
        send_loads(0, q, pair_sum(z, q))

    for copy in load_small:
        copy.wait()
    params[...] = jnp.zeros_like(params)
    for n, ref in enumerate((omega, damp)):
        mine = ref[...]
        none = jnp.zeros_like(mine)
        params[n, 0:33, :] = jnp.concatenate(
            [jnp.where(core == 0, mine, none), jnp.where(core == 1, mine, none)], 1
        )

    par_copy = pltpu.make_async_remote_copy(
        src_ref=params, dst_ref=params_in, send_sem=par_sem.at[0], recv_sem=par_sem.at[1],
        device_id=partner, device_id_type=MESH,
    )
    par_copy.start()

    ring_steps(1, longer)

    forward, _ = phase_values(0)
    fwd[...] = per_sample(forward)
    backward, weight = phase_values(1)
    inv[...] = per_sample(backward * weight)

    ring_steps(2, shorter)
    ring_steps(2, longer)

    par_copy.wait_recv()
    both = params[...] + params_in[...]
    freq = both[0, 0:33, :][:, None, :]
    ratio = both[1, 0:33, :][:, None, :]
    sample = lax.broadcasted_iota(jnp.int32, (GROUP, 256), 0)
    lane = lax.broadcasted_iota(jnp.int32, (GROUP, 256), 1)
    here = lane == core * 128 + col * GROUP + sample
    picked = jnp.where(here, harm[...].astype(F32), 0.0)
    drive = (0.25 * jnp.sum(picked, axis=1, keepdims=True))[None, :, :]
    stiff = freq * freq - drive * drive
    loss = 2.0 * ratio * freq * drive
    size = stiff * stiff + loss * loss
    for ref, value in ((recv_re, stiff / size), (recv_im, -loss / size)):
        ref[0:33] = value
        ref[33:64] = value[1:32]

    pl.semaphore_wait(ready, COLS - 1)
    for chunks in (shorter, longer):
        for n in range(2):
            for way in range(2):
                q = chunks[way][n]
                send_loads(way + 1, q, ring_sum(way, 3, q))

    all_arrived(loads_in.at[0, pl.ds(0, COLS - 1)], fwd_r.at[0])
    all_arrived(loads_in.at[1], fwd_r.at[1])
    all_arrived(loads_in.at[2], fwd_r.at[2])

    force = (
        loads_in[0].astype(F32) + loads_in[1].astype(F32) + loads_in[2].astype(F32)
    ).astype(BF16).reshape(512, LANES)
    wave = jnp.dot(fwd[...], force, preferred_element_type=F32)
    response = jnp.concatenate(
        [
            (wave * recv_re[...].reshape(512, LANES)).astype(BF16),
            (wave * recv_im[...].reshape(512, LANES)).astype(BF16),
        ],
        1,
    )
    back = jnp.dot(inv[...], response, preferred_element_type=F32)
    resp_out[...] = jnp.concatenate(
        [
            back[:, :LANES].reshape(SECTORS, GROUP, LANES),
            back[:, LANES:].reshape(SECTORS, GROUP, LANES),
        ],
        1,
    ).astype(BF16)

    def back_copy(kind, to, source):
        return pltpu.make_async_remote_copy(
            src_ref=resp_out.at[pl.ds(to * 4, 4)],
            dst_ref=gathered.at[z, core, source // 4, source % 4],
            send_sem=back_s.at[kind], recv_sem=back_r.at[kind, source // 4],
            device_id=(to, planes[kind]), device_id_type=MESH,
        )

    for step in (10, 9, 11, 6, 14, 5, 7, 13, 15, 2, 8, 1, 3, 4, 12, 0):
        to = (col + step) % COLS

        @pl.when(y < DIRECT)
        def _():
            back_copy(1, to, col).start()
            back_copy(2, to, col).start()

        if step:
            back_copy(0, to, col).start()
    gathered[z, core, y, col % 4] = resp_out[pl.ds(col * 4, 4)]

    def back_arrival(kind, q, count=4):
        block = at_z((0, -1, 1)[kind])
        all_arrived(gathered.at[block, core, q, pl.ds(0, count)], back_r.at[kind, q])

    def ag_slot(way, hop, q):
        first = 4 - DIRECT
        if hop == 1:
            slot = q - DIRECT
        elif hop < 4:
            slot = first + (hop - 2) * 4 + q
        else:
            slot = first + 8 + longer[way].index(q)
        return way * (first + 10) + slot

    def ag_copy(way, hop, q):
        block = at_z((1 - hop) * (1, -1)[way])
        return pltpu.make_async_remote_copy(
            src_ref=gathered.at[block, core, q], dst_ref=gathered.at[block, core, q],
            send_sem=ag_s.at[0], recv_sem=ag_r.at[ag_slot(way, hop, q)],
            device_id=beside[way], device_id_type=MESH,
        )

    def ag_arrival(way, hop, q):
        block = at_z(hop * (-1, 1)[way])
        return pltpu.make_async_remote_copy(
            src_ref=gathered.at[block, core, q], dst_ref=gathered.at[block, core, q],
            send_sem=ag_s.at[0], recv_sem=ag_r.at[ag_slot(way, hop, q)],
            device_id=beside[way], device_id_type=MESH,
        )

    def share(step, q, half):
        block = at_z(step)
        return pltpu.make_async_remote_copy(
            src_ref=gathered.at[block, half, q], dst_ref=gathered.at[block, half, q],
            send_sem=pair_s.at[0], recv_sem=pair_r.at[(abs(step) + 3) % 4, q],
            device_id=partner, device_id_type=MESH,
        )

    load_rec.wait()

    def task(hop, half, q):
        one, two = (at_z(-hop), at_z(hop)) if hop < 4 else (at_z(0), at_z(4))
        rows = pl.ds(pl.multiple_of(half * 128 + q * 32, 32), 32)

        left = jnp.concatenate([gathered[b, half, q].reshape(256, LANES) for b in (one, two)], 1)
        right = jnp.concatenate([rec[b] for b in (one, two)], 0)
        part = jnp.dot(left, right, preferred_element_type=F32)
        if hop == 1:
            total[half, q] = part
        elif hop < 4:
            total[half, q] += part
        else:
            stress = total[half, q] + part
            for s in range(4):
                for n, stage in enumerate((stage_re, stage_im)):
                    stage[s, rows, :] = jnp.concatenate(
                        [stress[o * 64 + s * 16 + n * 8 :][:8] for o in range(4)], 0
                    ).astype(BF16)

    def begin(q):
        @pl.when(y == q)
        def _():
            back_arrival(0, q, 3)

        @pl.when(y != q)
        def _():
            back_arrival(0, q)

        if q >= DIRECT:
            ag_copy(0, 1, q).start()
            ag_copy(1, 1, q).start()
        share(0, q, core).start()

    def arrive(hop, q):
        for way in range(2):
            if hop < 4 or q in longer[way]:
                if hop == 1 and q < DIRECT:
                    back_arrival(way + 1, q)
                else:
                    ag_arrival(way, hop, q).wait_recv()
                if hop < 3 or (hop == 3 and q in longer[way]):
                    ag_copy(way, hop + 1, q).start()
                share(hop * (-1, 1)[way] if hop < 4 else 4, q, core).start()

    def shared_task(hop, q):
        all_arrived(gathered.at[pl.ds(0, 2), other, q], pair_r.at[hop - 1, q])
        task(hop, other, q)

    begin(2)
    begin(3)
    pending = None
    for hop, q in (
        (1, 0), (1, 1), (0, 0), (0, 1), (1, 2), (1, 3), (2, 0), (2, 1), (2, 2), (2, 3),
        (3, 0), (3, 1), (3, 2), (3, 3), (4, 0), (4, 1), (4, 2), (4, 3),
    ):
        if hop == 0:
            begin(q)
            continue
        arrive(hop, q)
        task(hop, core, q)
        if pending is not None:
            shared_task(*pending)
        pending = (hop, q)
    shared_task(*pending)

    all_sent(give, give_s.at[0])
    par_copy.wait_send()
    all_sent(ring_out, ring_s.at[0])
    all_sent(loads_out.at[0, pl.ds(0, COLS - 1)], fwd_s.at[0])
    all_sent(resp_out.at[pl.ds(0, 4 * (COLS - 1))], back_s.at[0])
    for kind in (1, 2):
        all_sent(loads_out.at[kind], fwd_s.at[kind])

        @pl.when(y < DIRECT)
        def _():
            all_sent(resp_out, back_s.at[kind])

    all_sent(gathered.at[pl.ds(0, 4)], pair_s.at[0])
    all_sent(gathered.at[pl.ds(0, 7 - DIRECT // 2), 0], ag_s.at[0])


def write_out(stage_re, stage_im, out_re, out_im, sem):
    copies = [
        pltpu.make_async_copy(stage.at[s], out.at[s], sem.at[n, s])
        for n, (stage, out) in enumerate(((stage_re, out_re), (stage_im, out_im)))
        for s in range(4)
    ]
    for copy in copies:
        copy.start()
    for copy in copies:
        copy.wait()


def local(pressure, basis, recovery, omega, damping, harmonic):
    dma = pltpu.SemaphoreType.DMA
    anywhere = pl.BlockSpec(memory_space=pl.ANY)
    held = pl.BlockSpec(memory_space=pltpu.VMEM)
    out = jax.ShapeDtypeStruct((4, 256, 1024), BF16)
    stage = pltpu.VMEM((4, 256, 1024), BF16)
    staged = pl.pallas_call(
        kernel,
        out_shape=(stage, stage),
        in_specs=[anywhere] * 6,
        out_specs=(held, held),
        scratch_shapes=[
            pltpu.VMEM((4, 256, 1024), BF16),
            pltpu.VMEM((1024, 1024), BF16),
            pltpu.VMEM((8, 128, 1024), BF16),
            pltpu.VMEM((33, 64), F32),
            pltpu.VMEM((33, 64), F32),
            pltpu.VMEM((1, 256), jnp.int32),
            pltpu.VMEM((512, 512), BF16),
            pltpu.VMEM((512, 512), BF16),
            pltpu.VMEM((8, CHUNKS, 128, LANES), F32),
            pltpu.VMEM((8, CHUNKS, 128, LANES), BF16),
            pltpu.VMEM((8, CHUNKS, 128, LANES), BF16),
            pltpu.VMEM((2, 40, LANES), F32),
            pltpu.VMEM((2, 40, LANES), F32),
            pltpu.VMEM((SECTORS, GROUP, LANES), F32),
            pltpu.VMEM((SECTORS, GROUP, LANES), F32),
            pltpu.VMEM((20, 128, LANES), BF16),
            pltpu.VMEM((20, 128, LANES), BF16),
            pltpu.VMEM((3, COLS, 2, 16, LANES), BF16),
            pltpu.VMEM((3, COLS, 2, 16, LANES), BF16),
            pltpu.VMEM((SECTORS, 16, LANES), BF16),
            pltpu.VMEM((8, 2, CHUNKS, 4, 4, 16, LANES), BF16),
            pltpu.VMEM((2, CHUNKS, 256, 1024), F32),
            dma((10,)),
            dma((1,)), dma((8,)),
            dma((2,)),
            dma((1,)), dma((20,)),
            dma((3,)), dma((3,)),
            dma((3,)), dma((3, CHUNKS)),
            dma((1,)), dma((2 * (14 - DIRECT),)),
            dma((1,)), dma((4, CHUNKS)),
            pltpu.SemaphoreType.REGULAR,
        ],
        compiler_params=pltpu.CompilerParams(
            collective_id=0, has_side_effects=True, vmem_limit_bytes=52 * 2**20
        ),
        cost_estimate=pl.CostEstimate(
            flops=7 * 2**30, bytes_accessed=12 * 2**20, transcendentals=0
        ),
    )(
        *(
            pltpu.with_memory_space_constraint(array, pltpu.HBM)
            for array in (
                pressure, basis, recovery.reshape(8, 128, 1024), omega, damping,
                harmonic.reshape(1, 256),
            )
        )
    )
    return pl.pallas_call(
        write_out,
        out_shape=(out, out),
        in_specs=[anywhere, anywhere],
        out_specs=(anywhere, anywhere),
        scratch_shapes=[dma((2, 4))],
        compiler_params=pltpu.CompilerParams(vmem_limit_bytes=2**20),
    )(*(pltpu.with_memory_space_constraint(array, pltpu.VMEM) for array in staged))


def solution(mesh):
    in_specs = (
        P("sector", None, "mode"),
        P("mode", None),
        P(None, "mode"),
        P(None, "mode"),
        P(None, "mode"),
        P(),
    )
    out_specs = (P("sector", None, "mode"), P("sector", None, "mode"))
    return jax.shard_map(local, mesh=mesh, in_specs=in_specs, out_specs=out_specs, check_vma=False)
```

```python
import functools
import math

import jax
import jax.numpy as jnp
from jax import lax
from jax.experimental import pallas as pl
from jax.experimental.pallas import tpu as pltpu
from jax.sharding import PartitionSpec as P

MESH = pl.DeviceIdType.MESH
SECTORS = 64
COLS = 16
LANES = 128
GROUP = 8
CHUNKS = 4
DIRECT = 2
LATER = (2, 3)
F32 = jnp.float32
BF16 = jnp.bfloat16


def phase_values(diameter_dim):
    shape = (SECTORS, SECTORS)
    number = lax.broadcasted_iota(jnp.int32, shape, diameter_dim)
    sector = lax.broadcasted_iota(jnp.int32, shape, 1 - diameter_dim)
    half = SECTORS // 2
    sine = number > half
    diameter = jnp.where(sine, number - half, number)
    angle = (2.0 * math.pi / SECTORS) * ((diameter * sector) % SECTORS).astype(F32)
    value = jnp.where(sine, -jnp.sin(angle), jnp.cos(angle))
    once = (number == 0) | (number == half)
    return value, jnp.where(once, 1.0 / SECTORS, 2.0 / SECTORS)


def per_sample(table):
    size = SECTORS * GROUP
    rows = jnp.broadcast_to(table[:, None, :], (SECTORS, GROUP, SECTORS)).reshape(size, SECTORS)
    spread = (
        lax.broadcasted_iota(jnp.int32, (SECTORS, size), 0)
        == lax.broadcasted_iota(jnp.int32, (SECTORS, size), 1) // GROUP
    )
    wide = jnp.dot(
        rows.astype(BF16), spread.astype(F32).astype(BF16), preferred_element_type=F32
    )
    same = (
        lax.broadcasted_iota(jnp.int32, (size, size), 0) % GROUP
        == lax.broadcasted_iota(jnp.int32, (size, size), 1) % GROUP
    )
    return jnp.where(same, wide, 0.0).astype(BF16)


def kernel(
    press_hbm, basis_hbm, rec_hbm, omega_hbm, damp_hbm, harm_hbm,
    stage_re, stage_im, rest, last_left, last_right,
    press, basis, rec, omega, damp, harm, fwd, inv,
    own, give, take, params, params_in, recv_re, recv_im,
    ring_out, ring_in, loads_out, loads_in, resp_out, gathered, total,
    load_sem, give_s, give_r, par_sem, ring_s, ring_r, fwd_s, fwd_r, back_s, back_r,
    ag_s, ag_r, pair_s, pair_r, ready,
):
    col = lax.axis_index("sector")
    place = lax.axis_index("mode")
    z = place // 2
    core = place % 2
    other = 1 - core
    y = col // 4
    partner = (col, z * 2 + other)

    def at_z(step):
        return (z + step + 8) % 8

    up = (col, at_z(1) * 2 + core)
    down = (col, at_z(-1) * 2 + core)
    beside = (up, down)

    def samples(half):
        return pl.ds(pl.multiple_of(half * 128, 128), 128)

    load_press = [
        pltpu.make_async_copy(
            press_hbm.at[:, samples(half), :], press.at[:, samples(half), :], load_sem.at[n]
        )
        for n, half in enumerate((other, core))
    ]
    def load_basis(n):
        columns = pl.ds(n * 256 if isinstance(n, int) else pl.multiple_of(n * 256, 256), 256)
        return pltpu.make_async_copy(
            basis_hbm.at[:, columns], basis.at[:, columns], load_sem.at[2 + n]
        )

    load_small = [
        pltpu.make_async_copy(a, b, load_sem.at[6 + n])
        for n, (a, b) in enumerate(((omega_hbm, omega), (damp_hbm, damp), (harm_hbm, harm)))
    ]
    load_rec = pltpu.make_async_copy(rec_hbm, rec, load_sem.at[9])
    load_press[0].start()
    for n in range(4):
        load_basis(n).start()
    load_press[1].start()
    for copy in load_small:
        copy.start()

    barrier = pltpu.get_barrier_semaphore()
    for device in (up, down, partner):
        pl.semaphore_signal(barrier, inc=1, device_id=device, device_id_type=MESH)
    for step in range(1, COLS):
        pl.semaphore_signal(
            barrier, inc=1, device_id=((col + step) % COLS, place), device_id_type=MESH
        )

    def partial(half, target, n):
        part = jnp.dot(
            press[:, samples(half), :].reshape(512, 1024),
            basis[:, pl.ds(pl.multiple_of(n * 256, 256), 256)],
            preferred_element_type=F32,
        ).astype(target.dtype)
        for b in range(2):
            for q in range(CHUNKS):
                for s in range(4):
                    target[2 * n + b, q, s * 32 : s * 32 + 32, :] = part[
                        s * 128 + q * 32 : s * 128 + q * 32 + 32, b * 128 : b * 128 + 128
                    ]

    def give_tile(n, _):
        load_basis(n).wait()
        partial(other, give, n)
        return 0

    def own_tile(n, _):
        partial(core, own, (z // 2 + 2 + n) % 4)
        return 0

    load_press[0].wait()
    lax.fori_loop(0, 4, give_tile, 0)
    load_press[1].wait()
    pl.semaphore_wait(barrier, COLS + 2)

    def all_sent(ref, sem):
        pltpu.make_async_remote_copy(
            src_ref=ref, dst_ref=ref, send_sem=sem, recv_sem=sem,
            device_id=partner, device_id_type=MESH,
        ).wait_send()

    def all_arrived(ref, sem):
        pltpu.make_async_remote_copy(
            src_ref=ref, dst_ref=ref, send_sem=sem, recv_sem=sem,
            device_id=partner, device_id_type=MESH,
        ).wait_recv()

    def pair_copy(n, block):
        return pltpu.make_async_remote_copy(
            src_ref=give.at[block], dst_ref=take.at[block], send_sem=give_s.at[0],
            recv_sem=give_r.at[n], device_id=partner, device_id_type=MESH,
        )

    order = (4, 3, -3, 2, -2, 1, -1, 0)
    pair_copies = {}
    for n, step in enumerate(order):
        pair_copies[step] = pair_copy(n, at_z(step))
    pair_copies[4].start()

    for step in range(1, COLS):
        pl.semaphore_signal(
            ready, inc=1, device_id=((col + step) % COLS, place), device_id_type=MESH
        )
    load_rec.start()

    longer = ((0, 2), (1, 3))
    shorter = ((1, 3), (0, 2))

    def ring_slot(way, hop, q):
        return way * 10 + (longer[way].index(q) if hop == 0 else hop * 4 - 2 + q)

    def ring_copy(way, hop, q):
        slot = ring_slot(way, hop, q)
        return pltpu.make_async_remote_copy(
            src_ref=ring_out.at[slot], dst_ref=ring_in.at[slot],
            send_sem=ring_s.at[0], recv_sem=ring_r.at[slot],
            device_id=beside[way], device_id_type=MESH,
        )

    def pair_sum(block, q):
        return own[block, q] + take[block, q].astype(F32)

    def ring_sum(way, hop, q):
        value = pair_sum(at_z((4 - hop) * (1, -1)[way]), q)
        if hop > 1 or (hop == 1 and q in longer[way]):
            ring_copy(way, hop - 1, q).wait_recv()
            value = value + ring_in[ring_slot(way, hop - 1, q)].astype(F32)
        return value

    def ring_steps(hop, chunks):
        for n in range(2):
            for way in range(2):
                q = chunks[way][n]
                ring_out[ring_slot(way, hop, q)] = ring_sum(way, hop, q).astype(BF16)
                ring_copy(way, hop, q).start()

    planes = (place, at_z(1) * 2 + core, at_z(-1) * 2 + core)

    def fwd_copy(kind, to, source):
        return pltpu.make_async_remote_copy(
            src_ref=loads_out.at[kind, to], dst_ref=loads_in.at[kind, source],
            send_sem=fwd_s.at[kind], recv_sem=fwd_r.at[kind],
            device_id=(to, planes[kind]), device_id_type=MESH,
        )

    def send_loads(kind, q, force):
        for o in range(4):
            to = q * 4 + o
            for pair in range(2):
                at = 2 * pair * 32 + o * 8
                loads_out[kind, to, pair] = jnp.concatenate(
                    [force[at : at + 8], force[at + 32 : at + 40]], 0
                ).astype(BF16)
            if kind:
                fwd_copy(kind, to, col).start()
            else:

                @pl.when(to != col)
                def _():
                    fwd_copy(0, to, col).start()

                @pl.when(to == col)
                def _():
                    loads_in[0, col] = loads_out[0, col]

    lax.fori_loop(0, 1, own_tile, 0)
    for step in order[1:]:
        pair_copies[step].start()
    pair_copies[4].wait_recv()
    ring_steps(0, longer)
    lax.fori_loop(1, 4, own_tile, 0)
    for step in (3, -3):
        pair_copies[step].wait_recv()
    ring_steps(1, shorter)
    for step in (2, -2, 1, -1, 0):
        pair_copies[step].wait_recv()
    for q in range(CHUNKS):
        send_loads(0, q, pair_sum(z, q))

    for copy in load_small:
        copy.wait()
    params[...] = jnp.zeros_like(params)
    for n, ref in enumerate((omega, damp)):
        mine = ref[...]
        none = jnp.zeros_like(mine)
        params[n, 0:33, :] = jnp.concatenate(
            [jnp.where(core == 0, mine, none), jnp.where(core == 1, mine, none)], 1
        )

    par_copy = pltpu.make_async_remote_copy(
        src_ref=params, dst_ref=params_in, send_sem=par_sem.at[0], recv_sem=par_sem.at[1],
        device_id=partner, device_id_type=MESH,
    )
    par_copy.start()

    ring_steps(1, longer)

    forward, _ = phase_values(0)
    fwd[...] = per_sample(forward)
    backward, weight = phase_values(1)
    inv[...] = per_sample(backward * weight)

    ring_steps(2, shorter)
    ring_steps(2, longer)

    par_copy.wait_recv()
    both = params[...] + params_in[...]
    freq = both[0, 0:33, :][:, None, :]
    ratio = both[1, 0:33, :][:, None, :]
    sample = lax.broadcasted_iota(jnp.int32, (GROUP, 256), 0)
    lane = lax.broadcasted_iota(jnp.int32, (GROUP, 256), 1)
    here = lane == core * 128 + col * GROUP + sample
    picked = jnp.where(here, harm[...].astype(F32), 0.0)
    drive = (0.25 * jnp.sum(picked, axis=1, keepdims=True))[None, :, :]
    stiff = freq * freq - drive * drive
    loss = 2.0 * ratio * freq * drive
    size = stiff * stiff + loss * loss
    for ref, value in ((recv_re, stiff / size), (recv_im, -loss / size)):
        ref[0:33] = value
        ref[33:64] = value[1:32]

    pl.semaphore_wait(ready, COLS - 1)
    for chunks in (shorter, longer):
        for n in range(2):
            for way in range(2):
                q = chunks[way][n]
                send_loads(way + 1, q, ring_sum(way, 3, q))

    all_arrived(loads_in.at[0, pl.ds(0, COLS - 1)], fwd_r.at[0])
    all_arrived(loads_in.at[1], fwd_r.at[1])
    all_arrived(loads_in.at[2], fwd_r.at[2])

    force = (
        loads_in[0].astype(F32) + loads_in[1].astype(F32) + loads_in[2].astype(F32)
    ).astype(BF16).reshape(512, LANES)
    wave = jnp.dot(fwd[...], force, preferred_element_type=F32)
    response = jnp.concatenate(
        [
            (wave * recv_re[...].reshape(512, LANES)).astype(BF16),
            (wave * recv_im[...].reshape(512, LANES)).astype(BF16),
        ],
        1,
    )
    back = jnp.dot(inv[...], response, preferred_element_type=F32)
    resp_out[...] = jnp.concatenate(
        [
            back[:, :LANES].reshape(SECTORS, GROUP, LANES),
            back[:, LANES:].reshape(SECTORS, GROUP, LANES),
        ],
        1,
    ).astype(BF16)

    def back_copy(kind, to, source):
        return pltpu.make_async_remote_copy(
            src_ref=resp_out.at[pl.ds(to * 4, 4)],
            dst_ref=gathered.at[z, core, source // 4, source % 4],
            send_sem=back_s.at[kind], recv_sem=back_r.at[kind, source // 4],
            device_id=(to, planes[kind]), device_id_type=MESH,
        )

    for step in (10, 9, 11, 6, 14, 5, 7, 13, 15, 2, 8, 1, 3, 4, 12, 0):
        to = (col + step) % COLS

        @pl.when(y < DIRECT)
        def _():
            back_copy(1, to, col).start()
            back_copy(2, to, col).start()

        if step:
            back_copy(0, to, col).start()
    gathered[z, core, y, col % 4] = resp_out[pl.ds(col * 4, 4)]

    def back_arrival(kind, q, count=4):
        block = at_z((0, -1, 1)[kind])
        all_arrived(gathered.at[block, core, q, pl.ds(0, count)], back_r.at[kind, q])

    def ag_slot(way, hop, q):
        first = 4 - DIRECT
        if hop == 1:
            slot = q - DIRECT
        elif hop < 4:
            slot = first + (hop - 2) * 4 + q
        else:
            slot = first + 8 + longer[way].index(q)
        return way * (first + 10) + slot

    def ag_copy(way, hop, q):
        block = at_z((1 - hop) * (1, -1)[way])
        return pltpu.make_async_remote_copy(
            src_ref=gathered.at[block, core, q], dst_ref=gathered.at[block, core, q],
            send_sem=ag_s.at[0], recv_sem=ag_r.at[ag_slot(way, hop, q)],
            device_id=beside[way], device_id_type=MESH,
        )

    def ag_arrival(way, hop, q):
        block = at_z(hop * (-1, 1)[way])
        return pltpu.make_async_remote_copy(
            src_ref=gathered.at[block, core, q], dst_ref=gathered.at[block, core, q],
            send_sem=ag_s.at[0], recv_sem=ag_r.at[ag_slot(way, hop, q)],
            device_id=beside[way], device_id_type=MESH,
        )

    def share(step, q, half):
        block = at_z(step)
        return pltpu.make_async_remote_copy(
            src_ref=gathered.at[block, half, q], dst_ref=gathered.at[block, half, q],
            send_sem=pair_s.at[0], recv_sem=pair_r.at[(abs(step) + 3) % 4, q],
            device_id=partner, device_id_type=MESH,
        )

    load_rec.wait()

    def blocks(one, two, half, q):
        return jnp.concatenate([gathered[b, half, q].reshape(256, LANES) for b in (one, two)], 1)

    last_right[0:LANES, :] = rec[z]
    last_right[LANES:, :] = rec[at_z(4)]

    def task(hop, half, q):
        if hop == 4 and q in LATER:
            last_left[half, q - LATER[0]] = blocks(z, at_z(4), half, q)
            return
        if hop == 4:
            part = jnp.dot(
                blocks(z, at_z(4), half, q), last_right[...], preferred_element_type=F32
            )
            put_stress(total[half, q] + part, stage_re, stage_im, half, q)
            return
        one, two = at_z(-hop), at_z(hop)
        part = jnp.dot(
            blocks(one, two, half, q),
            jnp.concatenate([rec[b] for b in (one, two)], 0),
            preferred_element_type=F32,
        )
        target, row = (rest, q - LATER[0]) if q in LATER else (total, q)
        if hop == 1:
            target[half, row] = part
        else:
            target[half, row] += part

    def begin(q):
        @pl.when(y == q)
        def _():
            back_arrival(0, q, 3)

        @pl.when(y != q)
        def _():
            back_arrival(0, q)

        if q >= DIRECT:
            ag_copy(0, 1, q).start()
            ag_copy(1, 1, q).start()
        share(0, q, core).start()

    def arrive(hop, q):
        for way in range(2):
            if hop < 4 or q in longer[way]:
                if hop == 1 and q < DIRECT:
                    back_arrival(way + 1, q)
                else:
                    ag_arrival(way, hop, q).wait_recv()
                if hop < 3 or (hop == 3 and q in longer[way]):
                    ag_copy(way, hop + 1, q).start()
                share(hop * (-1, 1)[way] if hop < 4 else 4, q, core).start()

    def shared_task(hop, q):
        all_arrived(gathered.at[pl.ds(0, 2), other, q], pair_r.at[hop - 1, q])
        task(hop, other, q)

    begin(2)
    begin(3)
    pending = None
    for hop, q in (
        (1, 0), (1, 1), (0, 0), (0, 1), (1, 2), (1, 3), (2, 0), (2, 1), (2, 2), (2, 3),
        (3, 0), (3, 1), (3, 2), (3, 3), (4, 0), (4, 1), (4, 2), (4, 3),
    ):
        if hop == 0:
            begin(q)
            continue
        arrive(hop, q)
        task(hop, core, q)
        if pending is not None:
            shared_task(*pending)
        pending = (hop, q)
    shared_task(*pending)

    all_sent(give, give_s.at[0])
    par_copy.wait_send()
    all_sent(ring_out, ring_s.at[0])
    all_sent(loads_out.at[0, pl.ds(0, COLS - 1)], fwd_s.at[0])
    all_sent(resp_out.at[pl.ds(0, 4 * (COLS - 1))], back_s.at[0])
    for kind in (1, 2):
        all_sent(loads_out.at[kind], fwd_s.at[kind])

        @pl.when(y < DIRECT)
        def _():
            all_sent(resp_out, back_s.at[kind])

    all_sent(gathered.at[pl.ds(0, 4)], pair_s.at[0])
    all_sent(gathered.at[pl.ds(0, 7 - DIRECT // 2), 0], ag_s.at[0])


def put_stress(stress, stage_re, stage_im, half, place):
    start = half * (stage_re.shape[1] // 2) + place * 32
    if not isinstance(start, int):
        start = pl.multiple_of(start, 32)
    rows = pl.ds(start, 32)
    for s in range(4):
        for n, stage in enumerate((stage_re, stage_im)):
            stage[s, rows, :] = jnp.concatenate(
                [stress[o * 64 + s * 16 + n * 8 :][:8] for o in range(4)], 0
            ).astype(BF16)


def write_out(
    stage_re, stage_im, rest, last_left, last_right, out_re, out_im, late_re, late_im, sem
):
    early = 32 * LATER[0]
    copies = [
        pltpu.make_async_copy(
            stage.at[:, pl.ds(half * early, early), :],
            out.at[:, pl.ds(half * 128, early), :],
            sem.at[n, half, 0],
        )
        for n, (stage, out) in enumerate(((stage_re, out_re), (stage_im, out_im)))
        for half in range(2)
    ]
    for copy in copies:
        copy.start()
    for half in range(2):
        for row, q in enumerate(LATER):
            part = jnp.dot(last_left[half, row], last_right[...], preferred_element_type=F32)
            put_stress(rest[half, row] + part, late_re, late_im, half, row)
            for n, (stage, out) in enumerate(((late_re, out_re), (late_im, out_im))):
                copy = pltpu.make_async_copy(
                    stage.at[:, pl.ds(half * 32 * len(LATER) + row * 32, 32), :],
                    out.at[:, pl.ds(half * 128 + q * 32, 32), :],
                    sem.at[n, half, 1 + row],
                )
                copy.start()
                copies.append(copy)
    for copy in copies:
        copy.wait()


def local(pressure, basis, recovery, omega, damping, harmonic):
    dma = pltpu.SemaphoreType.DMA
    anywhere = pl.BlockSpec(memory_space=pl.ANY)
    held = pl.BlockSpec(memory_space=pltpu.VMEM)
    out = jax.ShapeDtypeStruct((4, 256, 1024), BF16)
    early, late = 64 * LATER[0], 64 * len(LATER)
    stage = pltpu.VMEM((4, early, 1024), BF16)
    staged = pl.pallas_call(
        kernel,
        out_shape=(
            stage, stage,
            pltpu.VMEM((2, len(LATER), 256, 1024), F32),
            pltpu.VMEM((2, len(LATER), 256, 2 * LANES), BF16),
            pltpu.VMEM((2 * LANES, 1024), BF16),
        ),
        in_specs=[anywhere] * 6,
        out_specs=(held,) * 5,
        scratch_shapes=[
            pltpu.VMEM((4, 256, 1024), BF16),
            pltpu.VMEM((1024, 1024), BF16),
            pltpu.VMEM((8, 128, 1024), BF16),
            pltpu.VMEM((33, 64), F32),
            pltpu.VMEM((33, 64), F32),
            pltpu.VMEM((1, 256), jnp.int32),
            pltpu.VMEM((512, 512), BF16),
            pltpu.VMEM((512, 512), BF16),
            pltpu.VMEM((8, CHUNKS, 128, LANES), F32),
            pltpu.VMEM((8, CHUNKS, 128, LANES), BF16),
            pltpu.VMEM((8, CHUNKS, 128, LANES), BF16),
            pltpu.VMEM((2, 40, LANES), F32),
            pltpu.VMEM((2, 40, LANES), F32),
            pltpu.VMEM((SECTORS, GROUP, LANES), F32),
            pltpu.VMEM((SECTORS, GROUP, LANES), F32),
            pltpu.VMEM((20, 128, LANES), BF16),
            pltpu.VMEM((20, 128, LANES), BF16),
            pltpu.VMEM((3, COLS, 2, 16, LANES), BF16),
            pltpu.VMEM((3, COLS, 2, 16, LANES), BF16),
            pltpu.VMEM((SECTORS, 16, LANES), BF16),
            pltpu.VMEM((8, 2, CHUNKS, 4, 4, 16, LANES), BF16),
            pltpu.VMEM((2, LATER[0], 256, 1024), F32),
            dma((10,)),
            dma((1,)), dma((8,)),
            dma((2,)),
            dma((1,)), dma((20,)),
            dma((3,)), dma((3,)),
            dma((3,)), dma((3, CHUNKS)),
            dma((1,)), dma((2 * (14 - DIRECT),)),
            dma((1,)), dma((4, CHUNKS)),
            pltpu.SemaphoreType.REGULAR,
        ],
        compiler_params=pltpu.CompilerParams(
            collective_id=0, has_side_effects=True, vmem_limit_bytes=52 * 2**20
        ),
        cost_estimate=pl.CostEstimate(
            flops=7 * 2**30, bytes_accessed=12 * 2**20, transcendentals=0
        ),
    )(
        *(
            pltpu.with_memory_space_constraint(array, pltpu.HBM)
            for array in (
                pressure, basis, recovery.reshape(8, 128, 1024), omega, damping,
                harmonic.reshape(1, 256),
            )
        )
    )
    return pl.pallas_call(
        write_out,
        out_shape=(out, out),
        in_specs=[held] * 5,
        out_specs=(anywhere, anywhere),
        scratch_shapes=[
            pltpu.VMEM((4, late, 1024), BF16), pltpu.VMEM((4, late, 1024), BF16),
            dma((2, 2, 1 + len(LATER))),
        ],
        compiler_params=pltpu.CompilerParams(vmem_limit_bytes=8 * 2**20),
    )(*(pltpu.with_memory_space_constraint(array, pltpu.VMEM) for array in staged))


def solution(mesh):
    in_specs = (
        P("sector", None, "mode"),
        P("mode", None),
        P(None, "mode"),
        P(None, "mode"),
        P(None, "mode"),
        P(),
    )
    out_specs = (P("sector", None, "mode"), P("sector", None, "mode"))
    return jax.shard_map(local, mesh=mesh, in_specs=in_specs, out_specs=out_specs, check_vma=False)
```

```python
import functools
import math

import jax
import jax.numpy as jnp
from jax import lax
from jax.experimental import pallas as pl
from jax.experimental.pallas import tpu as pltpu
from jax.sharding import PartitionSpec as P

MESH = pl.DeviceIdType.MESH
SECTORS = 64
COLS = 16
LANES = 128
GROUP = 8
CHUNKS = 4
DIRECT = 2
LATER = (2, 3)
F32 = jnp.float32
BF16 = jnp.bfloat16


def phase_values(diameter_dim):
    shape = (SECTORS, SECTORS)
    number = lax.broadcasted_iota(jnp.int32, shape, diameter_dim)
    sector = lax.broadcasted_iota(jnp.int32, shape, 1 - diameter_dim)
    half = SECTORS // 2
    sine = number > half
    diameter = jnp.where(sine, number - half, number)
    angle = (2.0 * math.pi / SECTORS) * ((diameter * sector) % SECTORS).astype(F32)
    value = jnp.where(sine, -jnp.sin(angle), jnp.cos(angle))
    once = (number == 0) | (number == half)
    return value, jnp.where(once, 1.0 / SECTORS, 2.0 / SECTORS)


def per_sample(table):
    size = SECTORS * GROUP
    rows = jnp.broadcast_to(table[:, None, :], (SECTORS, GROUP, SECTORS)).reshape(size, SECTORS)
    spread = (
        lax.broadcasted_iota(jnp.int32, (SECTORS, size), 0)
        == lax.broadcasted_iota(jnp.int32, (SECTORS, size), 1) // GROUP
    )
    wide = jnp.dot(
        rows.astype(BF16), spread.astype(F32).astype(BF16), preferred_element_type=F32
    )
    same = (
        lax.broadcasted_iota(jnp.int32, (size, size), 0) % GROUP
        == lax.broadcasted_iota(jnp.int32, (size, size), 1) % GROUP
    )
    return jnp.where(same, wide, 0.0).astype(BF16)


def kernel(
    press_hbm, basis_hbm, rec_hbm, omega_hbm, damp_hbm, harm_hbm,
    stage_re, stage_im, rest, last_left, last_right,
    press, basis, rec, omega, damp, harm, fwd, inv,
    own, give, take, params, params_in, recv_re, recv_im,
    ring_out, ring_in, loads_out, loads_in, resp_out, gathered, total,
    load_sem, give_s, give_r, par_sem, ring_s, ring_r, fwd_s, fwd_r, back_s, back_r,
    ag_s, ag_r, pair_r, ready,
):
    col = lax.axis_index("sector")
    place = lax.axis_index("mode")
    z = place // 2
    core = place % 2
    other = 1 - core
    y = col // 4
    partner = (col, z * 2 + other)

    def at_z(step):
        return (z + step + 8) % 8

    up = (col, at_z(1) * 2 + core)
    down = (col, at_z(-1) * 2 + core)
    beside = (up, down)

    def samples(half):
        return pl.ds(pl.multiple_of(half * 128, 128), 128)

    load_press = [
        pltpu.make_async_copy(
            press_hbm.at[:, samples(half), :], press.at[:, samples(half), :], load_sem.at[n]
        )
        for n, half in enumerate((other, core))
    ]
    def load_basis(n):
        columns = pl.ds(n * 256 if isinstance(n, int) else pl.multiple_of(n * 256, 256), 256)
        return pltpu.make_async_copy(
            basis_hbm.at[:, columns], basis.at[:, columns], load_sem.at[2 + n]
        )

    load_small = [
        pltpu.make_async_copy(a, b, load_sem.at[6 + n])
        for n, (a, b) in enumerate(((omega_hbm, omega), (damp_hbm, damp), (harm_hbm, harm)))
    ]
    load_rec = pltpu.make_async_copy(rec_hbm, rec, load_sem.at[9])
    load_press[0].start()
    for n in range(4):
        load_basis(n).start()
    load_press[1].start()
    for copy in load_small:
        copy.start()

    barrier = pltpu.get_barrier_semaphore()
    for device in (up, down, partner):
        pl.semaphore_signal(barrier, inc=1, device_id=device, device_id_type=MESH)
    for step in range(1, COLS):
        pl.semaphore_signal(
            barrier, inc=1, device_id=((col + step) % COLS, place), device_id_type=MESH
        )

    def partial(half, target, n):
        part = jnp.dot(
            press[:, samples(half), :].reshape(512, 1024),
            basis[:, pl.ds(pl.multiple_of(n * 256, 256), 256)],
            preferred_element_type=F32,
        ).astype(target.dtype)
        for b in range(2):
            for q in range(CHUNKS):
                for s in range(4):
                    target[2 * n + b, q, s * 32 : s * 32 + 32, :] = part[
                        s * 128 + q * 32 : s * 128 + q * 32 + 32, b * 128 : b * 128 + 128
                    ]

    def give_tile(n, _):
        load_basis(n).wait()
        partial(other, give, n)
        return 0

    def own_tile(n, _):
        partial(core, own, (z // 2 + 2 + n) % 4)
        return 0

    load_press[0].wait()
    lax.fori_loop(0, 4, give_tile, 0)
    load_press[1].wait()
    pl.semaphore_wait(barrier, COLS + 2)

    def all_sent(ref, sem):
        pltpu.make_async_remote_copy(
            src_ref=ref, dst_ref=ref, send_sem=sem, recv_sem=sem,
            device_id=partner, device_id_type=MESH,
        ).wait_send()

    def all_arrived(ref, sem):
        pltpu.make_async_remote_copy(
            src_ref=ref, dst_ref=ref, send_sem=sem, recv_sem=sem,
            device_id=partner, device_id_type=MESH,
        ).wait_recv()

    def pair_copy(n, block):
        return pltpu.make_async_remote_copy(
            src_ref=give.at[block], dst_ref=take.at[block], send_sem=give_s.at[0],
            recv_sem=give_r.at[(n + 1) // 2 if n < 3 else 2], device_id=partner, device_id_type=MESH,
        )

    order = (4, 3, -3, 2, -2, 1, -1, 0)
    pair_copies = {}
    for n, step in enumerate(order):
        pair_copies[step] = pair_copy(n, at_z(step))
    pair_copies[4].start()

    for step in range(1, COLS):
        pl.semaphore_signal(
            ready, inc=1, device_id=((col + step) % COLS, place), device_id_type=MESH
        )
    load_rec.start()

    longer = ((0, 2), (1, 3))
    shorter = ((1, 3), (0, 2))

    def ring_slot(way, hop, q):
        return way * 10 + (longer[way].index(q) if hop == 0 else hop * 4 - 2 + q)

    def ring_copy(way, hop, q):
        slot = ring_slot(way, hop, q)
        return pltpu.make_async_remote_copy(
            src_ref=ring_out.at[slot], dst_ref=ring_in.at[slot],
            send_sem=ring_s.at[0], recv_sem=ring_r.at[slot],
            device_id=beside[way], device_id_type=MESH,
        )

    def pair_sum(block, q):
        return own[block, q] + take[block, q].astype(F32)

    def ring_sum(way, hop, q):
        value = pair_sum(at_z((4 - hop) * (1, -1)[way]), q)
        if hop > 1 or (hop == 1 and q in longer[way]):
            ring_copy(way, hop - 1, q).wait_recv()
            value = value + ring_in[ring_slot(way, hop - 1, q)].astype(F32)
        return value

    def ring_steps(hop, chunks):
        for n in range(2):
            for way in range(2):
                q = chunks[way][n]
                ring_out[ring_slot(way, hop, q)] = ring_sum(way, hop, q).astype(BF16)
                ring_copy(way, hop, q).start()

    planes = (place, at_z(1) * 2 + core, at_z(-1) * 2 + core)

    def fwd_copy(kind, to, source):
        return pltpu.make_async_remote_copy(
            src_ref=loads_out.at[kind, to], dst_ref=loads_in.at[kind, source],
            send_sem=fwd_s.at[kind], recv_sem=fwd_r.at[kind],
            device_id=(to, planes[kind]), device_id_type=MESH,
        )

    def send_loads(kind, q, force):
        for o in range(4):
            to = q * 4 + o
            for pair in range(2):
                at = 2 * pair * 32 + o * 8
                loads_out[kind, to, pair] = jnp.concatenate(
                    [force[at : at + 8], force[at + 32 : at + 40]], 0
                ).astype(BF16)
            if kind:
                fwd_copy(kind, to, col).start()
            else:

                @pl.when(to != col)
                def _():
                    fwd_copy(0, to, col).start()

                @pl.when(to == col)
                def _():
                    loads_in[0, col] = loads_out[0, col]

    lax.fori_loop(0, 1, own_tile, 0)
    for step in order[1:]:
        pair_copies[step].start()
    all_arrived(take.at[0], give_r.at[0])
    ring_steps(0, longer)
    lax.fori_loop(1, 4, own_tile, 0)
    all_arrived(take.at[pl.ds(0, 2)], give_r.at[1])
    ring_steps(1, shorter)
    all_arrived(take.at[pl.ds(0, 5)], give_r.at[2])
    for q in range(CHUNKS):
        send_loads(0, q, pair_sum(z, q))

    for copy in load_small:
        copy.wait()
    params[...] = jnp.zeros_like(params)
    for n, ref in enumerate((omega, damp)):
        mine = ref[...]
        none = jnp.zeros_like(mine)
        params[n, 0:33, :] = jnp.concatenate(
            [jnp.where(core == 0, mine, none), jnp.where(core == 1, mine, none)], 1
        )

    par_copy = pltpu.make_async_remote_copy(
        src_ref=params, dst_ref=params_in, send_sem=par_sem.at[0], recv_sem=par_sem.at[1],
        device_id=partner, device_id_type=MESH,
    )
    par_copy.start()

    ring_steps(1, longer)

    forward, _ = phase_values(0)
    fwd[...] = per_sample(forward)
    backward, weight = phase_values(1)
    inv[...] = per_sample(backward * weight)

    ring_steps(2, shorter)
    ring_steps(2, longer)

    par_copy.wait_recv()
    both = params[...] + params_in[...]
    freq = both[0, 0:33, :][:, None, :]
    ratio = both[1, 0:33, :][:, None, :]
    sample = lax.broadcasted_iota(jnp.int32, (GROUP, 256), 0)
    lane = lax.broadcasted_iota(jnp.int32, (GROUP, 256), 1)
    here = lane == core * 128 + col * GROUP + sample
    picked = jnp.where(here, harm[...].astype(F32), 0.0)
    drive = (0.25 * jnp.sum(picked, axis=1, keepdims=True))[None, :, :]
    stiff = freq * freq - drive * drive
    loss = 2.0 * ratio * freq * drive
    size = stiff * stiff + loss * loss
    for ref, value in ((recv_re, stiff / size), (recv_im, -loss / size)):
        ref[0:33] = value
        ref[33:64] = value[1:32]

    pl.semaphore_wait(ready, COLS - 1)
    for chunks in (shorter, longer):
        for n in range(2):
            for way in range(2):
                q = chunks[way][n]
                send_loads(way + 1, q, ring_sum(way, 3, q))

    all_arrived(loads_in.at[0, pl.ds(0, COLS - 1)], fwd_r.at[0])
    all_arrived(loads_in.at[1], fwd_r.at[1])
    all_arrived(loads_in.at[2], fwd_r.at[2])

    force = (
        loads_in[0].astype(F32) + loads_in[1].astype(F32) + loads_in[2].astype(F32)
    ).astype(BF16).reshape(512, LANES)
    wave = jnp.dot(fwd[...], force, preferred_element_type=F32)
    response = jnp.concatenate(
        [
            (wave * recv_re[...].reshape(512, LANES)).astype(BF16),
            (wave * recv_im[...].reshape(512, LANES)).astype(BF16),
        ],
        1,
    )
    def back_copy(kind, to, source):
        return pltpu.make_async_remote_copy(
            src_ref=resp_out.at[pl.ds(to * 4, 4)],
            dst_ref=gathered.at[z, core, source // 4, source % 4],
            send_sem=back_s.at[kind], recv_sem=back_r.at[(0, 4, 6)[kind] + source // 4],
            device_id=(to, planes[kind]), device_id_type=MESH,
        )

    for half in range(2):
        back = jnp.dot(inv[half * 256 : half * 256 + 256], response, preferred_element_type=F32)
        resp_out[half * 32 : half * 32 + 32] = jnp.concatenate(
            [
                back[:, :LANES].reshape(SECTORS // 2, GROUP, LANES),
                back[:, LANES:].reshape(SECTORS // 2, GROUP, LANES),
            ],
            1,
        ).astype(BF16)
        for step in (5, 2, 6, 1, 7, 3, 4, 0):
            to = half * 8 + (col + step) % 8

            @pl.when(y < DIRECT)
            def _():
                back_copy(1, to, col).start()
                back_copy(2, to, col).start()

            @pl.when(to != col)
            def _():
                back_copy(0, to, col).start()

    gathered[z, core, y, col % 4] = resp_out[pl.ds(col * 4, 4)]

    def back_arrival(kind, q, count=4):
        block = at_z((0, -1, 1)[kind])
        all_arrived(gathered.at[block, core, q, pl.ds(0, count)], back_r.at[(0, 4, 6)[kind] + q])

    def ag_slot(way, hop, q):
        first = 4 - DIRECT
        if hop == 1:
            slot = q - DIRECT
        elif hop < 4:
            slot = first + (hop - 2) * 4 + q
        else:
            slot = first + 8 + longer[way].index(q)
        return way * (first + 10) + slot

    def ag_copy(way, hop, q):
        block = at_z((1 - hop) * (1, -1)[way])
        return pltpu.make_async_remote_copy(
            src_ref=gathered.at[block, core, q], dst_ref=gathered.at[block, core, q],
            send_sem=ag_s.at[0], recv_sem=ag_r.at[ag_slot(way, hop, q)],
            device_id=beside[way], device_id_type=MESH,
        )

    def ag_arrival(way, hop, q):
        block = at_z(hop * (-1, 1)[way])
        return pltpu.make_async_remote_copy(
            src_ref=gathered.at[block, core, q], dst_ref=gathered.at[block, core, q],
            send_sem=ag_s.at[0], recv_sem=ag_r.at[ag_slot(way, hop, q)],
            device_id=beside[way], device_id_type=MESH,
        )

    def share(step, q, half):
        block = at_z(step)
        return pltpu.make_async_remote_copy(
            src_ref=gathered.at[block, half, q], dst_ref=gathered.at[block, half, q],
            send_sem=ag_s.at[0], recv_sem=pair_r.at[(abs(step) + 3) % 4, q],
            device_id=partner, device_id_type=MESH,
        )

    load_rec.wait()

    def blocks(one, two, half, q):
        return jnp.concatenate([gathered[b, half, q].reshape(256, LANES) for b in (one, two)], 1)

    last_right[0:LANES, :] = rec[z]
    last_right[LANES:, :] = rec[at_z(4)]

    def task(hop, half, q):
        if hop == 4 and q in LATER:
            last_left[half, q - LATER[0]] = blocks(z, at_z(4), half, q)
            return
        if hop == 4:
            part = jnp.dot(
                blocks(z, at_z(4), half, q), last_right[...], preferred_element_type=F32
            )
            put_stress(total[half, q] + part, stage_re, stage_im, half, q)
            return
        one, two = at_z(-hop), at_z(hop)
        part = jnp.dot(
            blocks(one, two, half, q),
            jnp.concatenate([rec[b] for b in (one, two)], 0),
            preferred_element_type=F32,
        )
        target, row = (rest, q - LATER[0]) if q in LATER else (total, q)
        if hop == 1:
            target[half, row] = part
        else:
            target[half, row] += part

    def begin(q):
        @pl.when(y == q)
        def _():
            back_arrival(0, q, 3)

        @pl.when(y != q)
        def _():
            back_arrival(0, q)

        if q >= DIRECT:
            ag_copy(0, 1, q).start()
            ag_copy(1, 1, q).start()
        share(0, q, core).start()

    def arrive(hop, q):
        for way in range(2):
            if hop < 4 or q in longer[way]:
                if hop == 1 and q < DIRECT:
                    back_arrival(way + 1, q)
                else:
                    ag_arrival(way, hop, q).wait_recv()
                if hop < 3 or (hop == 3 and q in longer[way]):
                    ag_copy(way, hop + 1, q).start()
                share(hop * (-1, 1)[way] if hop < 4 else 4, q, core).start()

    def shared_task(hop, q):
        all_arrived(gathered.at[pl.ds(0, 2), other, q], pair_r.at[hop - 1, q])
        task(hop, other, q)

    begin(2)
    begin(3)
    pending = None
    for hop, q in (
        (1, 0), (1, 1), (0, 0), (0, 1), (1, 2), (1, 3), (2, 0), (2, 1), (2, 2), (2, 3),
        (3, 0), (3, 1), (3, 2), (3, 3), (4, 0), (4, 1), (4, 2), (4, 3),
    ):
        if hop == 0:
            begin(q)
            continue
        arrive(hop, q)
        task(hop, core, q)
        if pending is not None:
            shared_task(*pending)
        pending = (hop, q)
    shared_task(*pending)

    all_sent(give, give_s.at[0])
    par_copy.wait_send()
    all_sent(ring_out, ring_s.at[0])
    all_sent(loads_out.at[0, pl.ds(0, COLS - 1)], fwd_s.at[0])
    all_sent(resp_out.at[pl.ds(0, 4 * (COLS - 1))], back_s.at[0])
    for kind in (1, 2):
        all_sent(loads_out.at[kind], fwd_s.at[kind])

        @pl.when(y < DIRECT)
        def _():
            all_sent(resp_out, back_s.at[kind])

    all_sent(gathered.at[pl.ds(0, 7)], ag_s.at[0])


def put_stress(stress, stage_re, stage_im, half, place):
    start = half * (stage_re.shape[1] // 2) + place * 32
    if not isinstance(start, int):
        start = pl.multiple_of(start, 32)
    rows = pl.ds(start, 32)
    for s in range(4):
        for n, stage in enumerate((stage_re, stage_im)):
            stage[s, rows, :] = jnp.concatenate(
                [stress[o * 64 + s * 16 + n * 8 :][:8] for o in range(4)], 0
            ).astype(BF16)


def write_out(
    stage_re, stage_im, rest, last_left, last_right, out_re, out_im, late_re, late_im, sem
):
    early = 32 * LATER[0]
    copies = [
        pltpu.make_async_copy(
            stage.at[:, pl.ds(half * early, early), :],
            out.at[:, pl.ds(half * 128, early), :],
            sem.at[n, half, 0],
        )
        for n, (stage, out) in enumerate(((stage_re, out_re), (stage_im, out_im)))
        for half in range(2)
    ]
    for copy in copies:
        copy.start()
    for half in range(2):
        for row, q in enumerate(LATER):
            part = jnp.dot(last_left[half, row], last_right[...], preferred_element_type=F32)
            put_stress(rest[half, row] + part, late_re, late_im, half, row)
            for n, (stage, out) in enumerate(((late_re, out_re), (late_im, out_im))):
                copy = pltpu.make_async_copy(
                    stage.at[:, pl.ds(half * 32 * len(LATER) + row * 32, 32), :],
                    out.at[:, pl.ds(half * 128 + q * 32, 32), :],
                    sem.at[n, half, 1 + row],
                )
                copy.start()
                copies.append(copy)
    for copy in copies:
        copy.wait()


def local(pressure, basis, recovery, omega, damping, harmonic):
    dma = pltpu.SemaphoreType.DMA
    anywhere = pl.BlockSpec(memory_space=pl.ANY)
    held = pl.BlockSpec(memory_space=pltpu.VMEM)
    out = jax.ShapeDtypeStruct((4, 256, 1024), BF16)
    early, late = 64 * LATER[0], 64 * len(LATER)
    stage = pltpu.VMEM((4, early, 1024), BF16)
    staged = pl.pallas_call(
        kernel,
        out_shape=(
            stage, stage,
            pltpu.VMEM((2, len(LATER), 256, 1024), F32),
            pltpu.VMEM((2, len(LATER), 256, 2 * LANES), BF16),
            pltpu.VMEM((2 * LANES, 1024), BF16),
        ),
        in_specs=[anywhere] * 6,
        out_specs=(held,) * 5,
        scratch_shapes=[
            pltpu.VMEM((4, 256, 1024), BF16),
            pltpu.VMEM((1024, 1024), BF16),
            pltpu.VMEM((8, 128, 1024), BF16),
            pltpu.VMEM((33, 64), F32),
            pltpu.VMEM((33, 64), F32),
            pltpu.VMEM((1, 256), jnp.int32),
            pltpu.VMEM((512, 512), BF16),
            pltpu.VMEM((512, 512), BF16),
            pltpu.VMEM((8, CHUNKS, 128, LANES), F32),
            pltpu.VMEM((8, CHUNKS, 128, LANES), BF16),
            pltpu.VMEM((8, CHUNKS, 128, LANES), BF16),
            pltpu.VMEM((2, 40, LANES), F32),
            pltpu.VMEM((2, 40, LANES), F32),
            pltpu.VMEM((SECTORS, GROUP, LANES), F32),
            pltpu.VMEM((SECTORS, GROUP, LANES), F32),
            pltpu.VMEM((20, 128, LANES), BF16),
            pltpu.VMEM((20, 128, LANES), BF16),
            pltpu.VMEM((3, COLS, 2, 16, LANES), BF16),
            pltpu.VMEM((3, COLS, 2, 16, LANES), BF16),
            pltpu.VMEM((SECTORS, 16, LANES), BF16),
            pltpu.VMEM((8, 2, CHUNKS, 4, 4, 16, LANES), BF16),
            pltpu.VMEM((2, LATER[0], 256, 1024), F32),
            dma((10,)),
            dma((1,)), dma((3,)),
            dma((2,)),
            dma((1,)), dma((20,)),
            dma((3,)), dma((3,)),
            dma((3,)), dma((8,)),
            dma((1,)), dma((2 * (14 - DIRECT),)),
            dma((4, CHUNKS)),
            pltpu.SemaphoreType.REGULAR,
        ],
        compiler_params=pltpu.CompilerParams(
            collective_id=0, has_side_effects=True, vmem_limit_bytes=52 * 2**20
        ),
        cost_estimate=pl.CostEstimate(
            flops=7 * 2**30, bytes_accessed=12 * 2**20, transcendentals=0
        ),
    )(
        *(
            pltpu.with_memory_space_constraint(array, pltpu.HBM)
            for array in (
                pressure, basis, recovery.reshape(8, 128, 1024), omega, damping,
                harmonic.reshape(1, 256),
            )
        )
    )
    return pl.pallas_call(
        write_out,
        out_shape=(out, out),
        in_specs=[held] * 5,
        out_specs=(anywhere, anywhere),
        scratch_shapes=[
            pltpu.VMEM((4, late, 1024), BF16), pltpu.VMEM((4, late, 1024), BF16),
            dma((2, 2, 1 + len(LATER))),
        ],
        compiler_params=pltpu.CompilerParams(vmem_limit_bytes=8 * 2**20),
    )(*(pltpu.with_memory_space_constraint(array, pltpu.VMEM) for array in staged))


def solution(mesh):
    in_specs = (
        P("sector", None, "mode"),
        P("mode", None),
        P(None, "mode"),
        P(None, "mode"),
        P(None, "mode"),
        P(),
    )
    out_specs = (P("sector", None, "mode"), P("sector", None, "mode"))
    return jax.shard_map(local, mesh=mesh, in_specs=in_specs, out_specs=out_specs, check_vma=False)
```
